256 devices in a mesh: tm: 8 (over x, core), tile: 32 (over y, z).
Axes of the slice: x: 4, y: 4, z: 8, core: 2. Of those that a mesh axis runs over, the one named last changes fastest.
Arguments:
- features: bfloat16 [48, 96, 24, 512], P('tm', 'tile')
- frame_counts: int32 [8], P('tm'), may hold values from 2 to 6, as said below
- row_lengths: int32 [32], P('tile'), may hold values from 1 to 3, 64 in all
- norm_gain: float32 [512], replicated, may hold values from 0.5 to 2
- norm_shift: float32 [512], replicated, may hold values from -3 to 3
- conv_weight: bfloat16 [3, 3, 3, 512, 256], replicated, may hold values from -0.0546875 to 0.0546875
- conv_bias: float32 [256], replicated, may hold values from -3 to 3
Outputs:
- upscaled: bfloat16 [48, 192, 48, 256], P('tm', 'tile')
The draws below stay inside these ranges and needn't reach their ends.
Inputs may be any that keep to these rules, and one draw needn't show every extreme that they name: `frame_counts`: live frames are the first frame slots of each time block; some block is full. `row_lengths`: live latent rows are the first row slots of each tile; some tile is full.
All inputs are finite; a program needn't handle non-finite values. No bound on the sum of `row_lengths` on one device may be relied on, other than what follows from the above.
Results may differ from the reference program's by a relative error of at most 0.0046.
Values may be sent and summed in bfloat16 or wider, within the bound.
A program may use at most 128 MiB of HBM per device.

```python
import math
import jax
import jax.numpy as jnp
import numpy as np
from jax import lax

C_IN = 512
C_OUT = 256
GROUPS = 32
FD = 6
ROWS = 3
W = 24
N_TM = 8
N_TILE = 32


def draw_features(key, part):
    key = jax.random.fold_in(key, 11)
    first, second, third = jax.random.split(key, 3)
    frames = FD * N_TM
    height = ROWS * N_TILE
    shape = (frames, height, W, C_IN)
    frame_pos = jnp.arange(frames, dtype=jnp.float32) / frames
    row_pos = jnp.arange(height, dtype=jnp.float32) / height
    base = jax.random.normal(first, shape, jnp.float32)
    rising = 3.0
    ramp = jnp.power(rising, frame_pos)[:, None] * jnp.power(rising, row_pos)[None, :]
    channel_scale = jnp.exp(jax.random.uniform(second, (C_IN,), jnp.float32, math.log(0.3), math.log(3.0)))
    channel_shift = 0.5 * jax.random.normal(third, (C_IN,), jnp.float32)
    values = base * ramp[:, :, None, None] * channel_scale + channel_shift
    return values.astype(jnp.bfloat16)


def draw_frame_counts(key, part):
    key = jax.random.fold_in(key, 12)
    first, second = jax.random.split(key, 2)
    counts = jax.random.randint(first, (N_TM,), 2, FD + 1)
    chosen = jax.random.randint(second, (), 0, N_TM)
    return jnp.where(jnp.arange(N_TM) == chosen, FD, counts).astype(jnp.int32)


def split_up(count, total, most, skew):
    portions = [(1 << 20) // math.isqrt(grade ** skew) + 1 for grade in range(2, count + 1)]
    surplus, given = total - most - (count - 1), [1] * (count - 1)
    while surplus > 0:
        movable = [i for i in range(count - 1) if given[i] < most]
        whole, budget = sum([portions[i] for i in movable]), surplus
        for i in movable:
            more = min(most - given[i], max(1, budget * portions[i] // whole), surplus)
            given[i] = given[i] + more
            surplus = surplus - more
    return np.array([most] + given)


def ragged_sizes(stream_key, count, total, limit, skew):
    if count == 2:
        one = jax.random.randint(stream_key, (), max(1, total - limit), min(limit, total - 1) + 1)
        return jnp.stack([one, total - one])
    sizes = jnp.asarray(split_up(count, total, limit, skew), jnp.int32)
    pairs = (count - 1) // 2
    source_of, taker = sizes[1:1 + 2 * pairs:2], sizes[2:2 + 2 * pairs:2]
    room = jnp.minimum(source_of - 1, limit - taker)
    passed = jax.random.randint(jax.random.fold_in(stream_key, 1), (pairs,), 0, 1 << 20) % (room + 1)
    sizes = sizes.at[1:1 + 2 * pairs:2].set(source_of - passed).at[2:2 + 2 * pairs:2].set(taker + passed)
    return sizes[jax.random.permutation(jax.random.fold_in(stream_key, 2), count)]


def scatter_about(own_key, extent, spread, bound, kind=jnp.bfloat16):
    array = spread * jax.random.normal(own_key, extent, jnp.float32)
    return jnp.clip(array, min=-bound, max=bound).astype(kind)


def setup_inputs(seed: int = 0) -> dict:
    streams_of = jax.random.split(jax.random.key(seed), 8)
    return {
        "features": draw_features(jax.random.fold_in(streams_of[7], 71), 0),
        "frame_counts": draw_frame_counts(jax.random.fold_in(streams_of[7], 71), 0),
        "row_lengths": ragged_sizes(streams_of[2], N_TILE, N_TILE * ((ROWS + 1) // 2), ROWS, 2).astype(jnp.int32),
        "norm_gain": jnp.clip(jnp.exp(jax.random.uniform(streams_of[3], (C_IN,), jnp.float32, math.log(0.5), math.log(2.0))), 0.5, 2.0),
        "norm_shift": scatter_about(streams_of[4], (C_IN,), 0.5, 3.0, jnp.float32),
        "conv_weight": scatter_about(streams_of[5], (3, 3, 3, C_IN, C_OUT), (27 * C_IN) ** -0.5, 0.0546875),
        "conv_bias": scatter_about(streams_of[6], (C_OUT,), 0.5, 3.0, jnp.float32),
    }


EPSILON = 1e-06

def reference(features, frame_counts, row_lengths, norm_gain, norm_shift, conv_weight, conv_bias):
    frames = FD * N_TM
    height = ROWS * N_TILE
    width = W
    span = C_IN // GROUPS
    frame_index = jnp.arange(frames, dtype=jnp.int32)
    block_of = frame_index // FD
    within = frame_index % FD
    frame_live = within < frame_counts[block_of]
    row_index = jnp.arange(height, dtype=jnp.int32)
    tile_of = row_index // ROWS
    place = row_index % ROWS
    row_live = place < row_lengths[tile_of]
    mask = (frame_live[:, None] & row_live[None, :]).astype(jnp.float32)
    values = features.astype(jnp.float32).reshape(frames, height, width, GROUPS, span)
    weight_mask = mask[:, :, None, None, None]
    cells = jnp.sum(mask) * (width * span)
    mean = lax.optimization_barrier(jnp.sum(values * weight_mask, axis=(0, 1, 2, 4))) / cells
    centered = values - mean[:, None]
    variance = lax.optimization_barrier(jnp.sum(centered * centered * weight_mask, axis=(0, 1, 2, 4))) / cells
    normed = (centered * lax.rsqrt(variance + EPSILON)[:, None]).reshape(frames, height, width, C_IN)
    normed = normed * norm_gain.astype(jnp.float32) + norm_shift.astype(jnp.float32)
    hidden = jax.nn.silu(normed).astype(jnp.bfloat16)
    prior_block = jnp.maximum(block_of - 1, 0)
    earlier = jnp.where(within >= 1, frame_index - 1, jnp.where(block_of > 0, prior_block * FD + frame_counts[prior_block] - 1, frame_index))
    earliest = earlier[earlier]
    above_tile = jnp.maximum(tile_of - 1, 0)
    below_tile = jnp.minimum(tile_of + 1, N_TILE - 1)
    upper_row = jnp.where(place >= 1, row_index - 1, above_tile * ROWS + row_lengths[above_tile] - 1)
    upper_live = (place >= 1) | (tile_of > 0)
    last_place = place >= row_lengths[tile_of] - 1
    lower_row = jnp.where(last_place, below_tile * ROWS, row_index + 1)
    lower_live = jnp.logical_not(last_place) | (tile_of < N_TILE - 1)
    fine_rows = jnp.arange(2 * height, dtype=jnp.int32)
    coarse_row = fine_rows // 2
    row_parity = fine_rows % 2
    always = jnp.ones((2 * height,), dtype=bool)
    row_pick = [jnp.where(row_parity == 0, upper_row[coarse_row], coarse_row), coarse_row, jnp.where(row_parity == 1, lower_row[coarse_row], coarse_row)]
    row_keep = [jnp.where(row_parity == 0, upper_live[coarse_row], always), always, jnp.where(row_parity == 1, lower_live[coarse_row], always)]
    fine_cols = jnp.arange(2 * width, dtype=jnp.int32)
    coarse_col = fine_cols // 2
    col_parity = fine_cols % 2
    col_pick = [jnp.where(col_parity == 0, jnp.maximum(coarse_col - 1, 0), coarse_col), coarse_col, jnp.where(col_parity == 1, jnp.minimum(coarse_col + 1, width - 1), coarse_col)]
    col_keep = [(col_parity == 1) | (coarse_col > 0), jnp.ones((2 * width,), dtype=bool), (col_parity == 0) | (coarse_col < width - 1)]
    fine_live = row_live[coarse_row]

    def one_frame(frame):
        sources = (earliest[frame], earlier[frame], frame)
        total = jnp.zeros((4 * height * width, C_OUT), jnp.float32)
        for tdelta in range(3):
            plane = hidden[sources[tdelta]]
            for vertical in range(3):
                strip = plane[row_pick[vertical]] * row_keep[vertical].astype(hidden.dtype)[:, None, None]
                for horizontal in range(3):
                    patch = strip[:, col_pick[horizontal]] * col_keep[horizontal].astype(hidden.dtype)[None, :, None]
                    total = total + jnp.dot(patch.reshape(-1, C_IN), conv_weight[tdelta, vertical, horizontal], preferred_element_type=jnp.float32)
        result = total.reshape(2 * height, 2 * width, C_OUT) + conv_bias.astype(jnp.float32)
        keep = (fine_live & frame_live[frame]).astype(jnp.float32)
        return (result * keep[:, None, None]).astype(jnp.bfloat16)
    return lax.map(one_frame, frame_index)
```

```python
import functools

import jax
import jax.numpy as jnp
from jax import lax
from jax.experimental import pallas as pl
from jax.experimental.pallas import tpu as pltpu
from jax.sharding import PartitionSpec as P

GROUPS = 32
EPSILON = 1e-06
MESH = pl.DeviceIdType.MESH
LANES = 128
VMEM_LIMIT = 56 * 1024 * 1024


def group_matrix(channels, offset, transposed):
    span = channels // GROUPS
    shape = (LANES, channels) if transposed else (channels, LANES)
    channel = lax.broadcasted_iota(jnp.int32, shape, 1 if transposed else 0)
    lane = lax.broadcasted_iota(jnp.int32, shape, 0 if transposed else 1)
    low = (lane - offset) * span
    return ((channel >= low) & (channel < low + span)).astype(jnp.float32)


def exact_dot(a, b):
    return jnp.dot(a, b, precision=lax.Precision.HIGHEST, preferred_element_type=jnp.float32)


def merge(rows):
    totals = functools.reduce(lambda a, b: a + b, rows)
    counts = [pltpu.roll(row, LANES - 2 * GROUPS, 1) for row in rows]
    entries = pltpu.roll(totals, LANES - 2 * GROUPS, 1)
    mean = totals / entries
    between = jnp.zeros_like(totals)
    for row, count in zip(rows, counts):
        off = row / count - mean
        between = between + count * (off * off)
    spread = pltpu.roll(totals, LANES - GROUPS, 1) + between
    return totals, spread, entries


def as_row(totals, spread, entries):
    lane = lax.broadcasted_iota(jnp.int32, totals.shape, 1)
    spread = pltpu.roll(spread, GROUPS, 1)
    entries = pltpu.roll(entries, 2 * GROUPS, 1)
    row = jnp.where(lane < GROUPS, totals, jnp.where(lane < 2 * GROUPS, spread, entries))
    return jnp.where(lane < 3 * GROUPS, row, 1.0)


def exchange_kernel(
    dims, features, counts_in, lengths_in,
    stats, prior, upper, lower,
    block, tail, rising, sinking, first, second, counts, lengths,
    local_sems, send_sem, first_sem, second_sem, halo_sems,
):
    size_x, size_y, size_z, n_tm, n_tile = dims
    frames, height, width, channels = block.shape
    tm, tile = lax.axis_index("tm"), lax.axis_index("tile")
    x, core = tm // 2, tm % 2
    y, z = tile // size_z, tile % size_z

    def near(dz, dc):
        return (x * 2 + (core + dc) % 2, y * size_z + (z + dz) % size_z)

    def far(dx, dy):
        return (((x + dx) % size_x) * 2 + core, ((y + dy) % size_y) * size_z + z)

    def beside(dt, dr):
        return ((tm + dt + n_tm) % n_tm, (tile + dr + n_tile) % n_tile)

    near_steps = [(dz, dc) for dz in range(size_z) for dc in range(2)][1:]
    far_steps = [(dx, dy) for dx in range(size_x) for dy in range(size_y)][1:]
    halo_steps = [(a, b) for a in (-1, 0, 1) for b in (-1, 0, 1) if (a, b) != (0, 0)]

    load = pltpu.make_async_copy(features, block, local_sems.at[0])
    load.start()
    load_counts = pltpu.make_async_copy(counts_in, counts, local_sems.at[1])
    load_counts.start()
    load_lengths = pltpu.make_async_copy(lengths_in, lengths, local_sems.at[2])
    load_lengths.start()

    barrier = pltpu.get_barrier_semaphore()
    partners = [near(*s) for s in near_steps] + [far(*s) for s in far_steps]
    partners = partners + [beside(*s) for s in halo_steps]
    for partner in partners:
        pl.semaphore_signal(barrier, inc=1, device_id=partner, device_id_type=MESH)

    load_counts.wait()
    load_lengths.wait()
    load.wait()
    count_here = counts[0]
    length_here = lengths[0]

    recent = jnp.maximum(count_here - 2, 0)
    last_row = jnp.maximum(length_here - 1, 0)
    for k in range(2):
        tail[k] = block[recent + k]
        rising[k] = tail[k, last_row]
        sinking[k] = tail[k, 0]
    for k in range(frames):
        rising[2 + k] = block[k, last_row]
        sinking[2 + k] = block[k, 0]

    cells = (count_here * length_here * (width * (channels // GROUPS))).astype(jnp.float32)
    spread_out = group_matrix(channels, 0, True)
    gather = group_matrix(channels, 0, False)

    def over_live(term):
        total = jnp.zeros((8, channels), jnp.float32)
        for f in range(frames):
            for r in range(height):
                live = (f < count_here) & (r < length_here)
                part = term(block[f, r].astype(jnp.float32))
                part = jnp.where(live, part, 0.0)
                total = total + sum(part[8 * i : 8 * i + 8] for i in range(width // 8))
        return jnp.sum(exact_dot(total, gather), axis=0, keepdims=True)

    sums = over_live(lambda v: v)
    centre = exact_dot(jnp.broadcast_to(sums / cells, (8, LANES)), spread_out)[:1]
    spread = over_live(lambda v: (v - centre) * (v - centre))
    entries = jnp.zeros_like(sums) + cells
    first[0] = as_row(sums, spread, entries)

    pl.semaphore_wait(barrier, len(partners))

    copies = []

    def send(source, target, sem, device):
        copy = pltpu.make_async_remote_copy(
            src_ref=source, dst_ref=target, send_sem=send_sem, recv_sem=sem,
            device_id=device, device_id_type=MESH,
        )
        copy.start()
        return copy

    for i, step in enumerate(near_steps):
        send(first.at[0], first.at[1 + i], first_sem, near(*step))
    halos = [
        send(rising.at[pl.ds(2, frames)], upper.at[pl.ds(2, frames)], halo_sems.at[0], beside(0, 1)),
        send(sinking.at[pl.ds(2, frames)], lower.at[pl.ds(2, frames)], halo_sems.at[1], beside(0, -1)),
        send(rising.at[pl.ds(0, 2)], upper.at[pl.ds(0, 2)], halo_sems.at[2], beside(1, 1)),
        send(sinking.at[pl.ds(0, 2)], lower.at[pl.ds(0, 2)], halo_sems.at[3], beside(1, -1)),
        send(tail, prior, halo_sems.at[4], beside(1, 0)),
    ]

    arrived = first.at[pl.ds(1, len(near_steps))]
    pltpu.make_async_copy(arrived, arrived, first_sem).wait()
    second[0] = as_row(*merge([first[i] for i in range(1 + len(near_steps))]))
    for i, step in enumerate(far_steps):
        send(second.at[0], second.at[1 + i], second_sem, far(*step))
    arrived = second.at[pl.ds(1, len(far_steps))]
    pltpu.make_async_copy(arrived, arrived, second_sem).wait()
    totals, spread, entries = merge([second[i] for i in range(1 + len(far_steps))])
    mean = totals / entries
    scale = lax.rsqrt(spread / entries + EPSILON)
    both = jnp.concatenate([mean, scale, jnp.zeros((6, LANES), jnp.float32)], 0)
    lane = lax.broadcasted_iota(jnp.int32, both.shape, 1)
    stats[...] = exact_dot(jnp.where(lane < GROUPS, both, 0.0), spread_out)

    for halo in halos:
        halo.wait_recv()
    sent = first.at[pl.ds(1, len(near_steps))]
    pltpu.make_async_copy(sent, sent, send_sem).wait()
    sent = second.at[pl.ds(1, len(far_steps))]
    pltpu.make_async_copy(sent, sent, send_sem).wait()
    for halo in halos:
        halo.wait_send()


def convolve_kernel(
    n_tile, features, prior, upper, lower, weights, stats, gain, shift, bias, counts, lengths,
    out,
    raw, hidden, stacked, held, q0, q1, q2, rows, woven,
    raw_sem, weight_sems,
):
    frames, height, width, channels = features.shape
    slots = height + 2
    run = frames * width
    tm, tile = lax.axis_index("tm"), lax.axis_index("tile")
    count_here = counts[0]
    length_here = lengths[0]

    loads = []
    for r in range(height):
        loads.append((features.at[:, r], raw.at[1 + r, pl.ds(2, frames)]))
        loads.append((prior.at[:, r], raw.at[1 + r, pl.ds(0, 2)]))
    loads.append((upper, raw.at[0]))
    loads.append((lower, raw.at[slots - 1]))
    loads = [pltpu.make_async_copy(a, b, raw_sem.at[i]) for i, (a, b) in enumerate(loads)]
    for load in loads:
        load.start()
    order = [(v, h) for h in range(3) for v in range(3)]
    fetches = {}
    for v, h in order:
        i = v * 3 + h
        fetches[v, h] = pltpu.make_async_copy(weights.at[:, v, h], held.at[i], weight_sems.at[i])
        fetches[v, h].start()
    for load in loads:
        load.wait()

    mean = stats[0:1]
    scale = stats[1:2] * gain[...]
    offset = shift[...]
    for slot in range(slots):
        is_lower = slot == length_here + 1
        source = jnp.where(is_lower, slots - 1, slot)
        blank = (slot == 0) & (tile == 0) | is_lower & (tile == n_tile - 1)
        for k in range(frames + 2):
            frame = jnp.where(tm == 0, 2, k) if k < 2 else k
            v = raw[source, frame].astype(jnp.float32)
            v = (v - mean) * scale + offset
            v = v / (1.0 + jnp.exp(-v))
            hidden[pl.ds(k * width, width)] = jnp.where(blank, 0.0, v)
        for a in range(3):
            stacked[pl.ds(slot * run, run), pl.ds(a * channels, channels)] = hidden[
                pl.ds(a * width, run)
            ].astype(jnp.bfloat16)

    pad = 8
    for h in range(3):
        for v, q in enumerate((q0, q1, q2)):
            fetches[v, h].wait()
            depth = 3 * channels
            kernel = held[v * 3 + h].reshape(depth, held.shape[-1])
            start, size = (0 if v == 0 else run), (height if v == 1 else height + 1) * run
            q[pl.ds(0, size)] = jnp.dot(
                stacked[pl.ds(start, size)], kernel, preferred_element_type=jnp.float32
            )
        for r in range(height):
            here, after = pl.ds(r * run, run), pl.ds((r + 1) * run, run)
            middle = q1[here]
            rows[h, 0, pl.ds(pad + r * run, run)] = middle + q0[here] + q2[here]
            rows[h, 1, pl.ds(pad + r * run, run)] = middle + q0[after] + q2[after]

    column = lax.broadcasted_iota(jnp.int32, (width, 1), 0)
    for r in range(height):
        for s in range(2):
            for t in range(frames):
                at = pad + r * run + t * width
                left = jnp.where(column == 0, 0.0, rows[0, s, pl.ds(at - 1, width)])
                right = jnp.where(column == width - 1, 0.0, rows[2, s, pl.ds(at + 1, width)])
                base = rows[1, s, pl.ds(at, width)] + bias[...]
                even = base + left + rows[2, s, pl.ds(at, width)]
                odd = base + right + rows[0, s, pl.ds(at, width)]
                live = (t < count_here) & (r < length_here)
                slab = (2 * r + s) * frames + t
                even, odd = jnp.where(live, even, 0.0), jnp.where(live, odd, 0.0)
                for i in range(even.shape[-1] // LANES):
                    lanes = slice(i * LANES, (i + 1) * LANES)
                    woven[slab, i, pl.ds(0, width, 2)] = even[:, lanes]
                    woven[slab, i, pl.ds(1, width, 2)] = odd[:, lanes]
                    out[t, 2 * r + s, :, lanes] = woven[slab, i].astype(jnp.bfloat16)


def body(dims, features, frame_counts, row_lengths, norm_gain, norm_shift, conv_weight, conv_bias):
    frames, height, width, channels = features.shape
    made = conv_weight.shape[-1]
    size_x, size_y, size_z, n_tm, n_tile = dims
    anywhere = pl.BlockSpec(memory_space=pl.ANY)
    in_vmem = pl.BlockSpec(memory_space=pltpu.VMEM)
    in_smem = pl.BlockSpec(memory_space=pltpu.SMEM)
    bf16, f32 = jnp.bfloat16, jnp.float32
    halo = (frames + 2, width, channels)
    stats, prior, upper, lower = pl.pallas_call(
        functools.partial(exchange_kernel, dims),
        out_shape=(
            jax.ShapeDtypeStruct((8, channels), f32),
            jax.ShapeDtypeStruct((2, height, width, channels), bf16),
            jax.ShapeDtypeStruct(halo, bf16),
            jax.ShapeDtypeStruct(halo, bf16),
        ),
        in_specs=[anywhere] * 3,
        out_specs=(in_vmem, anywhere, anywhere, anywhere),
        scratch_shapes=[
            pltpu.VMEM(features.shape, bf16),
            pltpu.VMEM((2, height, width, channels), bf16),
            pltpu.VMEM(halo, bf16),
            pltpu.VMEM(halo, bf16),
            pltpu.VMEM((size_z * 2, 1, LANES), f32),
            pltpu.VMEM((size_x * size_y, 1, LANES), f32),
            pltpu.SMEM((1,), jnp.int32),
            pltpu.SMEM((1,), jnp.int32),
            pltpu.SemaphoreType.DMA((3,)),
            pltpu.SemaphoreType.DMA,
            pltpu.SemaphoreType.DMA,
            pltpu.SemaphoreType.DMA,
            pltpu.SemaphoreType.DMA((5,)),
        ],
        compiler_params=pltpu.CompilerParams(
            collective_id=0, has_side_effects=True, vmem_limit_bytes=16 * 1024 * 1024
        ),
        name="exchange",
    )(features, frame_counts, row_lengths)

    run = frames * width
    slots = height + 2
    return pl.pallas_call(
        functools.partial(convolve_kernel, n_tile),
        out_shape=jax.ShapeDtypeStruct((frames, 2 * height, 2 * width, made), bf16),
        in_specs=[anywhere] * 5 + [in_vmem] * 4 + [in_smem] * 2,
        out_specs=in_vmem,
        scratch_shapes=[
            pltpu.VMEM((slots, frames + 2, width, channels), bf16),
            pltpu.VMEM(((frames + 2) * width, channels), f32),
            pltpu.VMEM((slots * run, 3 * channels), bf16),
            pltpu.VMEM((9, 3, channels, made), bf16),
            pltpu.VMEM(((height + 1) * run, made), f32),
            pltpu.VMEM((height * run, made), f32),
            pltpu.VMEM(((height + 1) * run, made), f32),
            pltpu.VMEM((3, 2, height * run + 16, made), f32),
            pltpu.VMEM((2 * height * frames, made // LANES, 2 * width, LANES), f32),
            pltpu.SemaphoreType.DMA((2 * height + 2,)),
            pltpu.SemaphoreType.DMA((9,)),
        ],
        compiler_params=pltpu.CompilerParams(vmem_limit_bytes=VMEM_LIMIT),
        name="convolve",
    )(
        features, prior, upper, lower, conv_weight, stats,
        norm_gain.reshape(1, channels), norm_shift.reshape(1, channels),
        conv_bias.reshape(1, made), frame_counts, row_lengths,
    )


def factors(mesh):
    n_tm, n_tile = mesh.shape["tm"], mesh.shape["tile"]
    size_y = 1
    while size_y * size_y * 2 < n_tile:
        size_y *= 2
    return n_tm // 2, size_y, n_tile // size_y, n_tm, n_tile


def solution(mesh):
    in_specs = (P("tm", "tile", None, None), P("tm"), P("tile"), P(), P(), P(), P())
    out_specs = P("tm", "tile", None, None)
    return jax.shard_map(
        functools.partial(body, factors(mesh)),
        mesh=mesh, in_specs=in_specs, out_specs=out_specs, check_vma=False,
    )
```

```python
import functools

import jax
import jax.numpy as jnp
from jax import lax
from jax.experimental import pallas as pl
from jax.experimental.pallas import tpu as pltpu
from jax.sharding import PartitionSpec as P

GROUPS = 32
EPSILON = 1e-06
MESH = pl.DeviceIdType.MESH
LANES = 128
EXCHANGE_VMEM = 48 * 1024 * 1024
CONVOLVE_VMEM = 40 * 1024 * 1024


def group_matrix(channels, offset, transposed):
    span = channels // GROUPS
    shape = (LANES, channels) if transposed else (channels, LANES)
    channel = lax.broadcasted_iota(jnp.int32, shape, 1 if transposed else 0)
    lane = lax.broadcasted_iota(jnp.int32, shape, 0 if transposed else 1)
    low = (lane - offset) * span
    return ((channel >= low) & (channel < low + span)).astype(jnp.float32)


def exact_dot(a, b):
    return jnp.dot(a, b, precision=lax.Precision.HIGHEST, preferred_element_type=jnp.float32)


def merge(rows):
    totals = functools.reduce(lambda a, b: a + b, rows)
    counts = [pltpu.roll(row, LANES - 2 * GROUPS, 1) for row in rows]
    entries = pltpu.roll(totals, LANES - 2 * GROUPS, 1)
    mean = totals / entries
    between = jnp.zeros_like(totals)
    for row, count in zip(rows, counts):
        off = row / count - mean
        between = between + count * (off * off)
    spread = pltpu.roll(totals, LANES - GROUPS, 1) + between
    return totals, spread, entries


def as_row(totals, spread, entries):
    lane = lax.broadcasted_iota(jnp.int32, totals.shape, 1)
    spread = pltpu.roll(spread, GROUPS, 1)
    entries = pltpu.roll(entries, 2 * GROUPS, 1)
    row = jnp.where(lane < GROUPS, totals, jnp.where(lane < 2 * GROUPS, spread, entries))
    return jnp.where(lane < 3 * GROUPS, row, 1.0)


def exchange_kernel(
    dims, features, weights_in, gain_in, shift_in, bias_in, counts, lengths,
    block, prior, upper, lower, stats, weights, gain, shift, bias,
    tail, rising, sinking, first, second,
    local_sems, send_sem, first_sem, second_sem, halo_sems,
):
    size_x, size_y, size_z, n_tm, n_tile = dims
    frames, height, width, channels = block.shape
    tm, tile = lax.axis_index("tm"), lax.axis_index("tile")
    x, core = tm // 2, tm % 2
    y, z = tile // size_z, tile % size_z

    def near(dz, dc):
        return (x * 2 + (core + dc) % 2, y * size_z + (z + dz) % size_z)

    def far(dx, dy):
        return (((x + dx) % size_x) * 2 + core, ((y + dy) % size_y) * size_z + z)

    def beside(dt, dr):
        return ((tm + dt + n_tm) % n_tm, (tile + dr + n_tile) % n_tile)

    near_steps = [(dz, dc) for dz in range(size_z) for dc in range(2)][1:]
    far_steps = [(dx, dy) for dx in range(size_x) for dy in range(size_y)][1:]
    halo_steps = [(a, b) for a in (-1, 0, 1) for b in (-1, 0, 1) if (a, b) != (0, 0)]

    load = pltpu.make_async_copy(features, block, local_sems.at[0])
    load.start()

    barrier = pltpu.get_barrier_semaphore()
    partners = [near(*s) for s in near_steps] + [far(*s) for s in far_steps]
    partners = partners + [beside(*s) for s in halo_steps]
    for partner in partners:
        pl.semaphore_signal(barrier, inc=1, device_id=partner, device_id_type=MESH)

    ahead = [(weights_in, weights), (gain_in, gain), (shift_in, shift), (bias_in, bias)]
    ahead = [pltpu.make_async_copy(a, b, local_sems.at[1 + i]) for i, (a, b) in enumerate(ahead)]
    for copy in ahead:
        copy.start()

    load.wait()
    count_here = counts[0]
    length_here = lengths[0]

    recent = jnp.maximum(count_here - 2, 0)
    last_row = jnp.maximum(length_here - 1, 0)
    for k in range(2):
        tail[k] = block[recent + k]
        rising[k] = tail[k, last_row]
        sinking[k] = tail[k, 0]
    for k in range(frames):
        rising[2 + k] = block[k, last_row]
        sinking[2 + k] = block[k, 0]

    cells = (count_here * length_here * (width * (channels // GROUPS))).astype(jnp.float32)
    spread_out = group_matrix(channels, 0, True)
    gather = group_matrix(channels, 0, False)

    def over_live(term):
        total = jnp.zeros((8, channels), jnp.float32)
        for f in range(frames):
            for r in range(height):
                live = (f < count_here) & (r < length_here)
                part = term(block[f, r].astype(jnp.float32))
                part = jnp.where(live, part, 0.0)
                total = total + sum(part[8 * i : 8 * i + 8] for i in range(width // 8))
        return jnp.sum(exact_dot(total, gather), axis=0, keepdims=True)

    sums = over_live(lambda v: v)
    centre = exact_dot(jnp.broadcast_to(sums / cells, (8, LANES)), spread_out)[:1]
    spread = over_live(lambda v: (v - centre) * (v - centre))
    entries = jnp.zeros_like(sums) + cells
    first[0] = as_row(sums, spread, entries)

    pl.semaphore_wait(barrier, len(partners))

    def send(source, target, sem, device):
        copy = pltpu.make_async_remote_copy(
            src_ref=source, dst_ref=target, send_sem=send_sem, recv_sem=sem,
            device_id=device, device_id_type=MESH,
        )
        copy.start()
        return copy

    for i, step in enumerate(near_steps):
        send(first.at[0], first.at[1 + i], first_sem, near(*step))
    halos = [
        send(rising.at[pl.ds(2, frames)], upper.at[pl.ds(2, frames)], halo_sems.at[0], beside(0, 1)),
        send(sinking.at[pl.ds(2, frames)], lower.at[pl.ds(2, frames)], halo_sems.at[1], beside(0, -1)),
        send(rising.at[pl.ds(0, 2)], upper.at[pl.ds(0, 2)], halo_sems.at[2], beside(1, 1)),
        send(sinking.at[pl.ds(0, 2)], lower.at[pl.ds(0, 2)], halo_sems.at[3], beside(1, -1)),
        send(tail, prior, halo_sems.at[4], beside(1, 0)),
    ]

    arrived = first.at[pl.ds(1, len(near_steps))]
    pltpu.make_async_copy(arrived, arrived, first_sem).wait()
    second[0] = as_row(*merge([first[i] for i in range(1 + len(near_steps))]))
    for i, step in enumerate(far_steps):
        send(second.at[0], second.at[1 + i], second_sem, far(*step))
    arrived = second.at[pl.ds(1, len(far_steps))]
    pltpu.make_async_copy(arrived, arrived, second_sem).wait()
    totals, spread, entries = merge([second[i] for i in range(1 + len(far_steps))])
    mean = totals / entries
    scale = lax.rsqrt(spread / entries + EPSILON)
    both = jnp.concatenate([mean, scale, jnp.zeros((6, LANES), jnp.float32)], 0)
    lane = lax.broadcasted_iota(jnp.int32, both.shape, 1)
    stats[...] = exact_dot(jnp.where(lane < GROUPS, both, 0.0), spread_out)

    for copy in ahead:
        copy.wait()
    for halo in halos:
        halo.wait_recv()
    sent = first.at[pl.ds(1, len(near_steps))]
    pltpu.make_async_copy(sent, sent, send_sem).wait()
    sent = second.at[pl.ds(1, len(far_steps))]
    pltpu.make_async_copy(sent, sent, send_sem).wait()
    for halo in halos:
        halo.wait_send()


def convolve_kernel(
    n_tile, features, prior, upper, lower, stats, weights, gain, shift, bias, counts, lengths,
    out,
    hidden, stacked, q0, q1, q2, rows, woven,
):
    frames, height, width, channels = features.shape
    slots = height + 2
    run = frames * width
    tm, tile = lax.axis_index("tm"), lax.axis_index("tile")
    count_here = counts[0]
    length_here = lengths[0]
    mean = stats[0:1]
    scale = stats[1:2] * gain[...]
    offset = shift[...]
    for slot in range(slots):
        is_lower = slot == length_here + 1
        blank = (slot == 0) & (tile == 0) | is_lower & (tile == n_tile - 1)
        for k in range(frames + 2):
            frame = jnp.where(tm == 0, 2, k) if k < 2 else k
            if slot == 0: v = upper[frame]
            elif slot == slots - 1: v = lower[frame]
            else:
                v = prior[k, slot - 1] if k < 2 else features[k - 2, slot - 1]
                if k < 2:
                    v = jnp.where(tm == 0, features[0, slot - 1], v)
                if slot > 1:
                    v = jnp.where(is_lower, lower[frame], v)
            v = v.astype(jnp.float32)
            v = (v - mean) * scale + offset
            v = v / (1.0 + jnp.exp(-v))
            hidden[pl.ds(k * width, width)] = jnp.where(blank, 0.0, v)
        for a in range(3):
            stacked[pl.ds(slot * run, run), pl.ds(a * channels, channels)] = hidden[
                pl.ds(a * width, run)
            ].astype(jnp.bfloat16)

    pad = 8
    for h in range(3):
        for v, q in enumerate((q0, q1, q2)):
            depth = 3 * channels
            kernel = weights[:, v, h].reshape(depth, weights.shape[-1])
            start, size = (0 if v == 0 else run), (height if v == 1 else height + 1) * run
            q[pl.ds(0, size)] = jnp.dot(
                stacked[pl.ds(start, size)], kernel, preferred_element_type=jnp.float32
            )
        for r in range(height):
            here, after = pl.ds(r * run, run), pl.ds((r + 1) * run, run)
            middle = q1[here]
            rows[h, 0, pl.ds(pad + r * run, run)] = middle + q0[here] + q2[here]
            rows[h, 1, pl.ds(pad + r * run, run)] = middle + q0[after] + q2[after]

    column = lax.broadcasted_iota(jnp.int32, (width, 1), 0)
    for r in range(height):
        for s in range(2):
            for t in range(frames):
                at = pad + r * run + t * width
                left = jnp.where(column == 0, 0.0, rows[0, s, pl.ds(at - 1, width)])
                right = jnp.where(column == width - 1, 0.0, rows[2, s, pl.ds(at + 1, width)])
                base = rows[1, s, pl.ds(at, width)] + bias[...]
                even = base + left + rows[2, s, pl.ds(at, width)]
                odd = base + right + rows[0, s, pl.ds(at, width)]
                live = (t < count_here) & (r < length_here)
                slab = (2 * r + s) * frames + t
                even, odd = jnp.where(live, even, 0.0), jnp.where(live, odd, 0.0)
                for i in range(even.shape[-1] // LANES):
                    lanes = slice(i * LANES, (i + 1) * LANES)
                    woven[slab, i, pl.ds(0, width, 2)] = even[:, lanes]
                    woven[slab, i, pl.ds(1, width, 2)] = odd[:, lanes]
                    out[t, 2 * r + s, :, lanes] = woven[slab, i].astype(jnp.bfloat16)


def body(dims, features, frame_counts, row_lengths, norm_gain, norm_shift, conv_weight, conv_bias):
    frames, height, width, channels = features.shape
    made = conv_weight.shape[-1]
    size_x, size_y, size_z, n_tm, n_tile = dims
    run = frames * width
    anywhere = pl.BlockSpec(memory_space=pl.ANY)
    in_vmem = pl.BlockSpec(memory_space=pltpu.VMEM)
    in_smem = pl.BlockSpec(memory_space=pltpu.SMEM)
    bf16, f32 = jnp.bfloat16, jnp.float32
    halo = (frames + 2, width, channels)
    ready = pl.pallas_call(
        functools.partial(exchange_kernel, dims),
        out_shape=(
            pltpu.VMEM(features.shape, bf16),
            pltpu.VMEM((2, height, width, channels), bf16),
            pltpu.VMEM(halo, bf16),
            pltpu.VMEM(halo, bf16),
            pltpu.VMEM((8, channels), f32),
            pltpu.VMEM(conv_weight.shape, bf16),
            pltpu.VMEM((1, channels), f32),
            pltpu.VMEM((1, channels), f32),
            pltpu.VMEM((1, made), f32),
        ),
        in_specs=[anywhere] * 5 + [in_smem] * 2,
        out_specs=(in_vmem,) * 9,
        scratch_shapes=[
            pltpu.VMEM((2, height, width, channels), bf16),
            pltpu.VMEM(halo, bf16),
            pltpu.VMEM(halo, bf16),
            pltpu.VMEM((size_z * 2, 1, LANES), f32),
            pltpu.VMEM((size_x * size_y, 1, LANES), f32),
            pltpu.SemaphoreType.DMA((5,)),
            pltpu.SemaphoreType.DMA,
            pltpu.SemaphoreType.DMA,
            pltpu.SemaphoreType.DMA,
            pltpu.SemaphoreType.DMA((5,)),
        ],
        compiler_params=pltpu.CompilerParams(
            collective_id=0, has_side_effects=True, vmem_limit_bytes=EXCHANGE_VMEM
        ),
        name="exchange",
    )(
        features, conv_weight, norm_gain.reshape(1, channels), norm_shift.reshape(1, channels),
        conv_bias.reshape(1, made), frame_counts, row_lengths,
    )
    return pl.pallas_call(
        functools.partial(convolve_kernel, n_tile),
        out_shape=jax.ShapeDtypeStruct((frames, 2 * height, 2 * width, made), bf16),
        in_specs=[in_vmem] * 9 + [in_smem] * 2,
        out_specs=in_vmem,
        scratch_shapes=[
            pltpu.VMEM(((frames + 2) * width, channels), f32),
            pltpu.VMEM(((height + 2) * run, 3 * channels), bf16),
            pltpu.VMEM(((height + 1) * run, made), f32),
            pltpu.VMEM((height * run, made), f32),
            pltpu.VMEM(((height + 1) * run, made), f32),
            pltpu.VMEM((3, 2, height * run + 16, made), f32),
            pltpu.VMEM((2 * height * frames, made // LANES, 2 * width, LANES), f32),
        ],
        compiler_params=pltpu.CompilerParams(vmem_limit_bytes=CONVOLVE_VMEM),
        name="convolve",
    )(*ready, frame_counts, row_lengths)


def factors(mesh):
    n_tm, n_tile = mesh.shape["tm"], mesh.shape["tile"]
    size_y = 1
    while size_y * size_y * 2 < n_tile:
        size_y *= 2
    return n_tm // 2, size_y, n_tile // size_y, n_tm, n_tile


def solution(mesh):
    in_specs = (P("tm", "tile", None, None), P("tm"), P("tile"), P(), P(), P(), P())
    out_specs = P("tm", "tile", None, None)
    return jax.shard_map(
        functools.partial(body, factors(mesh)),
        mesh=mesh, in_specs=in_specs, out_specs=out_specs, check_vma=False,
    )
```

```python
import functools

import jax
import jax.numpy as jnp
from jax import lax
from jax.experimental import pallas as pl
from jax.experimental.pallas import tpu as pltpu
from jax.sharding import PartitionSpec as P

GROUPS = 32
EPSILON = 1e-06
MESH = pl.DeviceIdType.MESH
LANES = 128
EXCHANGE_VMEM = 48 * 1024 * 1024
CONVOLVE_VMEM = 40 * 1024 * 1024


def group_matrix(channels, offset, transposed):
    span = channels // GROUPS
    shape = (LANES, channels) if transposed else (channels, LANES)
    channel = lax.broadcasted_iota(jnp.int32, shape, 1 if transposed else 0)
    lane = lax.broadcasted_iota(jnp.int32, shape, 0 if transposed else 1)
    low = (lane - offset) * span
    return ((channel >= low) & (channel < low + span)).astype(jnp.float32)


def exact_dot(a, one_hot):
    high = a.astype(jnp.bfloat16).astype(jnp.float32)
    rest = a - high
    middle = rest.astype(jnp.bfloat16).astype(jnp.float32)
    terms = jnp.concatenate([high, middle, rest - middle, jnp.zeros_like(a)], 0).astype(jnp.bfloat16)
    out = jnp.dot(terms, one_hot.astype(jnp.bfloat16), preferred_element_type=jnp.float32)
    return out[:8] + out[8:16] + out[16:24]


def merge(rows):
    totals = functools.reduce(lambda a, b: a + b, rows)
    counts = [pltpu.roll(row, LANES - 2 * GROUPS, 1) for row in rows]
    entries = pltpu.roll(totals, LANES - 2 * GROUPS, 1)
    mean = totals / entries
    between = jnp.zeros_like(totals)
    for row, count in zip(rows, counts):
        off = row / count - mean
        between = between + count * (off * off)
    spread = pltpu.roll(totals, LANES - GROUPS, 1) + between
    return totals, spread, entries


def as_row(totals, spread, entries):
    lane = lax.broadcasted_iota(jnp.int32, totals.shape, 1)
    spread = pltpu.roll(spread, GROUPS, 1)
    entries = pltpu.roll(entries, 2 * GROUPS, 1)
    row = jnp.where(lane < GROUPS, totals, jnp.where(lane < 2 * GROUPS, spread, entries))
    return jnp.where(lane < 3 * GROUPS, row, 1.0)


def exchange_kernel(
    dims, features, weights_in, gain_in, shift_in, bias_in, counts, lengths,
    block, prior, upper, lower, stats, weights, gain, shift, bias,
    tail, rising, sinking, row, first, second, result,
    local_sems, row_send, first_sem, second_send, second_sem, result_send, result_sem,
    halo_send, halo_sems,
):
    size_x, size_y, size_z, n_tm, n_tile = dims
    frames, height, width, channels = block.shape
    tm, tile = lax.axis_index("tm"), lax.axis_index("tile")
    x, core = tm // 2, tm % 2
    y, z = tile // size_z, tile % size_z
    planes, half = size_z // 2, size_z // 4
    gathers = z < planes
    serves = ((z == 1) | (z == planes - 1)) & (core == 1)
    server = jnp.where(z < planes + half, planes - 1, 1)

    def column(other_z, other_core):
        return x * 2 + other_core, y * size_z + other_z

    def far(dx, dy):
        return ((x + dx) % size_x) * 2 + core, ((y + dy) % size_y) * size_z + z

    def beside(dt, dr):
        return (tm + dt + n_tm) % n_tm, (tile + dr + n_tile) % n_tile

    far_steps = [(dx, dy) for dx in range(size_x) for dy in range(size_y)][1:]
    halo_steps = [(a, b) for a in (-1, 0, 1) for b in (-1, 0, 1) if (a, b) != (0, 0)]
    n_column, n_gather = 2 * size_z, 2 * planes

    load = pltpu.make_async_copy(features, block, local_sems.at[0])
    load.start()

    barrier = pltpu.get_barrier_semaphore()

    def greet(device):
        pl.semaphore_signal(barrier, inc=1, device_id=device, device_id_type=MESH)

    for step in halo_steps:
        greet(beside(*step))

    @pl.when(gathers)
    def _():
        for dz in range(size_z):
            for dc in range(2):
                if dz + dc:
                    greet(column((z + dz) % size_z, (core + dc) % 2))
        for step in far_steps:
            greet(far(*step))

    @pl.when(jnp.logical_not(gathers))
    def _():
        greet(column(server, 1))

    ahead = [(weights_in, weights), (gain_in, gain), (shift_in, shift), (bias_in, bias)]
    ahead = [pltpu.make_async_copy(a, b, local_sems.at[1 + i]) for i, (a, b) in enumerate(ahead)]
    for copy in ahead:
        copy.start()

    load.wait()
    count_here = counts[0]
    length_here = lengths[0]

    cells = (count_here * length_here * (width * (channels // GROUPS))).astype(jnp.float32)
    spread_out = group_matrix(channels, 0, True)
    gather = group_matrix(channels, 0, False)

    def over_live(term):
        total = jnp.zeros((8, channels), jnp.float32)
        for f in range(frames):
            for r in range(height):
                live = (f < count_here) & (r < length_here)
                part = term(block[f, r].astype(jnp.float32))
                part = jnp.where(live, part, 0.0)
                total = total + sum(part[8 * i : 8 * i + 8] for i in range(width // 8))
        return jnp.sum(exact_dot(total, gather), axis=0, keepdims=True)

    sums = over_live(lambda v: v)
    centre = exact_dot(jnp.broadcast_to(sums / cells, (8, LANES)), spread_out)[:1]
    spread = over_live(lambda v: (v - centre) * (v - centre))
    entries = jnp.zeros_like(sums) + cells
    row[0] = as_row(sums, spread, entries)
    own = z * 2 + core

    def send_row(device):
        pltpu.make_async_remote_copy(
            src_ref=row.at[0], dst_ref=first.at[own], send_sem=row_send, recv_sem=first_sem,
            device_id=device, device_id_type=MESH,
        ).start()

    @pl.when(gathers)
    def _():
        known = n_gather - 1 + len(far_steps) + len(halo_steps)
        pl.semaphore_wait(barrier, known + jnp.where(serves, 4, 0))
        first[own] = row[0]
        for dz in range(planes):
            for dc in range(2):
                if dz + dc:
                    send_row(column((z + dz) % planes, (core + dc) % 2))

    @pl.when(jnp.logical_not(gathers))
    def _():
        pl.semaphore_wait(barrier, n_gather + len(halo_steps))
        for to_z in range(planes):
            for to_core in range(2):
                send_row(column(to_z, to_core))

    recent = jnp.maximum(count_here - 2, 0)
    last_row = jnp.maximum(length_here - 1, 0)
    for k in range(2):
        tail[k] = block[recent + k]
        rising[k] = tail[k, last_row]
        sinking[k] = tail[k, 0]
    for k in range(frames):
        rising[2 + k] = block[k, last_row]
        sinking[2 + k] = block[k, 0]
    here, before = pl.ds(2, frames), pl.ds(0, 2)
    halos = [
        (rising.at[here], upper.at[here], (0, 1)),
        (sinking.at[here], lower.at[here], (0, -1)),
        (rising.at[before], upper.at[before], (1, 1)),
        (sinking.at[before], lower.at[before], (1, -1)),
        (tail, prior, (1, 0)),
    ]
    halos = [
        pltpu.make_async_remote_copy(
            src_ref=source, dst_ref=target, send_sem=halo_send.at[i], recv_sem=halo_sems.at[i],
            device_id=beside(*step), device_id_type=MESH,
        )
        for i, (source, target, step) in enumerate(halos)
    ]
    for halo in halos:
        halo.start()
    widen = group_matrix(channels, 0, True) + group_matrix(channels, GROUPS, True)

    def answers():
        base = jnp.where(z == 1, planes + half, planes)
        return [
            pltpu.make_async_remote_copy(
                src_ref=result.at[0], dst_ref=result.at[0], send_sem=result_send.at[k],
                recv_sem=result_sem, device_id=column(base + k // 2, k % 2), device_id_type=MESH,
            )
            for k in range(4)
        ]

    @pl.when(gathers)
    def _():
        sent = first.at[pl.ds(0, n_gather - 1)]
        pltpu.make_async_copy(sent, sent, row_send).wait()
        arrived = first.at[pl.ds(0, n_column - 1)]
        pltpu.make_async_copy(arrived, arrived, first_sem).wait()
        second[0] = as_row(*merge([first[i] for i in range(n_column)]))
        copies = [
            pltpu.make_async_remote_copy(
                src_ref=second.at[0], dst_ref=second.at[1 + i], send_sem=second_send,
                recv_sem=second_sem, device_id=far(*step), device_id_type=MESH,
            )
            for i, step in enumerate(far_steps)
        ]
        for copy in copies:
            copy.start()
        for copy in ahead:
            copy.wait()
        for halo in halos:
            halo.wait()
        sent = second.at[pl.ds(1, len(far_steps))]
        pltpu.make_async_copy(sent, sent, second_send).wait()
        pltpu.make_async_copy(sent, sent, second_sem).wait()
        totals, spread, entries = merge([second[i] for i in range(1 + len(far_steps))])
        mean = totals / entries
        scale = lax.rsqrt(spread / entries + EPSILON)
        lane = lax.broadcasted_iota(jnp.int32, mean.shape, 1)
        result[0] = jnp.where(lane < GROUPS, mean, pltpu.roll(scale, GROUPS, 1))

        @pl.when(serves)
        def _():
            for answer in answers():
                answer.start()

    @pl.when(jnp.logical_not(gathers))
    def _():
        sent = first.at[pl.ds(0, n_gather)]
        pltpu.make_async_copy(sent, sent, row_send).wait()
        for copy in ahead:
            copy.wait()
        for halo in halos:
            halo.wait()
        pltpu.make_async_copy(result.at[0], result.at[0], result_sem).wait()

    both = jnp.broadcast_to(result[0], (8, LANES))
    lane = lax.broadcasted_iota(jnp.int32, both.shape, 1)
    sub = lax.broadcasted_iota(jnp.int32, both.shape, 0)
    stats[...] = exact_dot(jnp.where(lane // GROUPS == sub, both, 0.0), widen)

    @pl.when(serves)
    def _():
        for answer in answers():
            answer.wait_send()


def convolve_kernel(
    n_tile, features, prior, upper, lower, stats, weights, gain, shift, bias, counts, lengths,
    out_hbm,
    out, stacked, q0, q1, q2, woven, hidden, out_sems,
):
    frames, height, width, channels = features.shape
    slots, run, depth = height + 2, frames * width, 3 * channels
    products = (q0, q1, q2)
    tm, tile = lax.axis_index("tm"), lax.axis_index("tile")
    count_here = counts[0]
    length_here = lengths[0]
    mean = stats[0:1]
    scale = stats[1:2] * gain[...]
    offset = shift[...]
    column = lax.broadcasted_iota(jnp.int32, (width, 1), 0)

    def normalise(slot, k):
        is_lower = slot == length_here + 1
        blank = (slot == 0) & (tile == 0) | is_lower & (tile == n_tile - 1)
        frame = jnp.where(tm == 0, 2, k) if k < 2 else k
        if slot == 0:
            v = upper[frame]
        elif slot == slots - 1:
            v = lower[frame]
        else:
            v = prior[k, slot - 1] if k < 2 else features[k - 2, slot - 1]
            if k < 2:
                v = jnp.where(tm == 0, features[0, slot - 1], v)
            if slot > 1:
                v = jnp.where(is_lower, lower[frame], v)
        v = v.astype(jnp.float32)
        v = (v - mean) * scale + offset
        v = v / (1.0 + jnp.exp(-v))
        hidden[slot % 2, pl.ds(k * width, width)] = jnp.where(blank, 0.0, v)

    def stack(slot, a):
        stacked[pl.ds(slot * run, run), pl.ds(a * channels, channels)] = hidden[
            slot % 2, pl.ds(a * width, run)
        ].astype(jnp.bfloat16)

    def multiply(slot, h, v):
        kernel = weights[:, v, h].reshape(depth, weights.shape[-1])
        products[v][h, slot] = jnp.dot(
            stacked[pl.ds(slot * run, run)], kernel, preferred_element_type=jnp.float32
        )

    def finish(r, s, t):
        at = pl.ds(t * width, width)
        first, middle, last = [
            q0[h, r + s, at] + q1[h, r + 1, at] + q2[h, r + 1 + s, at] for h in range(3)
        ]
        middle = middle + bias[...]
        left = jnp.where(column == 0, 0.0, pltpu.roll(first, 1, 0))
        right = jnp.where(column == width - 1, 0.0, pltpu.roll(last, width - 1, 0))
        live = (t < count_here) & (r < length_here)
        even = jnp.where(live, middle + left + last, 0.0)
        odd = jnp.where(live, middle + right + first, 0.0)
        slab = (2 * r + s) * frames + t
        for i in range(even.shape[-1] // LANES):
            lanes = slice(i * LANES, (i + 1) * LANES)
            woven[slab, i, pl.ds(0, width, 2)] = even[:, lanes]
            woven[slab, i, pl.ds(1, width, 2)] = odd[:, lanes]
            out[t, 2 * r + s, :, lanes] = woven[slab, i].astype(jnp.bfloat16)

    def leave(row):
        return pltpu.make_async_copy(out.at[:, row], out_hbm.at[:, row], out_sems.at[row])

    def preparing(slot):
        work = [functools.partial(normalise, slot, k) for k in range(frames + 2)]
        return work + [functools.partial(stack, slot, a) for a in range(3)]

    def finishing(r, s):
        work = [functools.partial(finish, r, s, t) for t in range(frames)]
        return work + [lambda: leave(2 * r + s).start()]

    for piece in preparing(0):
        piece()
    for slot in range(slots):
        beside = preparing(slot + 1) if slot + 1 < slots else []
        if 2 <= slot:
            beside = beside + finishing(slot - 2, 0)
        if 3 <= slot:
            beside = finishing(slot - 3, 1) + beside
        taps = [
            (h, v) for h in range(3) for v in range(3)
            if not (slot == 0 and v > 0 or slot == slots - 1 and v < 2)
        ]
        done = 0
        for i, (h, v) in enumerate(taps):
            multiply(slot, h, v)
            upto = len(beside) * (i + 1) // len(taps)
            for piece in beside[done:upto]:
                piece()
            done = upto
    for piece in finishing(height - 1, 1):
        piece()
    for row in range(2 * height):
        leave(row).wait()


def body(dims, features, frame_counts, row_lengths, norm_gain, norm_shift, conv_weight, conv_bias):
    frames, height, width, channels = features.shape
    made = conv_weight.shape[-1]
    size_x, size_y, size_z, n_tm, n_tile = dims
    run = frames * width
    anywhere = pl.BlockSpec(memory_space=pl.ANY)
    in_vmem = pl.BlockSpec(memory_space=pltpu.VMEM)
    in_smem = pl.BlockSpec(memory_space=pltpu.SMEM)
    bf16, f32 = jnp.bfloat16, jnp.float32
    halo = (frames + 2, width, channels)
    ready = pl.pallas_call(
        functools.partial(exchange_kernel, dims),
        out_shape=(
            pltpu.VMEM(features.shape, bf16),
            pltpu.VMEM((2, height, width, channels), bf16),
            pltpu.VMEM(halo, bf16),
            pltpu.VMEM(halo, bf16),
            pltpu.VMEM((8, channels), f32),
            pltpu.VMEM(conv_weight.shape, bf16),
            pltpu.VMEM((1, channels), f32),
            pltpu.VMEM((1, channels), f32),
            pltpu.VMEM((1, made), f32),
        ),
        in_specs=[anywhere] * 5 + [in_smem] * 2,
        out_specs=(in_vmem,) * 9,
        scratch_shapes=[
            pltpu.VMEM((2, height, width, channels), bf16),
            pltpu.VMEM(halo, bf16),
            pltpu.VMEM(halo, bf16),
            pltpu.VMEM((1, 1, LANES), f32),
            pltpu.VMEM((size_z * 2, 1, LANES), f32),
            pltpu.VMEM((size_x * size_y, 1, LANES), f32),
            pltpu.VMEM((1, 1, LANES), f32),
            pltpu.SemaphoreType.DMA((5,)),
            pltpu.SemaphoreType.DMA,
            pltpu.SemaphoreType.DMA,
            pltpu.SemaphoreType.DMA,
            pltpu.SemaphoreType.DMA,
            pltpu.SemaphoreType.DMA((4,)),
            pltpu.SemaphoreType.DMA,
            pltpu.SemaphoreType.DMA((5,)),
            pltpu.SemaphoreType.DMA((5,)),
        ],
        compiler_params=pltpu.CompilerParams(
            collective_id=0, has_side_effects=True, vmem_limit_bytes=EXCHANGE_VMEM
        ),
        name="exchange",
    )(
        features, conv_weight, norm_gain.reshape(1, channels), norm_shift.reshape(1, channels),
        conv_bias.reshape(1, made), frame_counts, row_lengths,
    )
    return pl.pallas_call(
        functools.partial(convolve_kernel, n_tile),
        out_shape=jax.ShapeDtypeStruct((frames, 2 * height, 2 * width, made), bf16),
        in_specs=[in_vmem] * 9 + [in_smem] * 2,
        out_specs=anywhere,
        scratch_shapes=[
            pltpu.VMEM((frames, 2 * height, 2 * width, made), bf16),
            pltpu.VMEM(((height + 2) * run, 3 * channels), bf16),
            pltpu.VMEM((3, height + 2, run, made), f32),
            pltpu.VMEM((3, height + 2, run, made), f32),
            pltpu.VMEM((3, height + 2, run, made), f32),
            pltpu.VMEM((2 * height * frames, made // LANES, 2 * width, LANES), f32),
            pltpu.VMEM((2, (frames + 2) * width, channels), f32),
            pltpu.SemaphoreType.DMA((2 * height,)),
        ],
        compiler_params=pltpu.CompilerParams(vmem_limit_bytes=CONVOLVE_VMEM),
        name="convolve",
    )(*ready, frame_counts, row_lengths)


def factors(mesh):
    n_tm, n_tile = mesh.shape["tm"], mesh.shape["tile"]
    size_y = 1
    while size_y * size_y * 2 < n_tile:
        size_y *= 2
    return n_tm // 2, size_y, n_tile // size_y, n_tm, n_tile


def solution(mesh):
    in_specs = (P("tm", "tile", None, None), P("tm"), P("tile"), P(), P(), P(), P())
    out_specs = P("tm", "tile", None, None)
    return jax.shard_map(
        functools.partial(body, factors(mesh)),
        mesh=mesh, in_specs=in_specs, out_specs=out_specs, check_vma=False,
    )
```

```python
import functools

import jax
import jax.numpy as jnp
from jax import lax
from jax.experimental import pallas as pl
from jax.experimental.pallas import tpu as pltpu
from jax.sharding import PartitionSpec as P

GROUPS = 32
REACH = 1
EPSILON = 1e-06
MESH = pl.DeviceIdType.MESH
LANES = 128
EXCHANGE_VMEM = 48 * 1024 * 1024
CONVOLVE_VMEM = 40 * 1024 * 1024


def group_matrix(channels, offset, transposed):
    span = channels // GROUPS
    shape = (LANES, channels) if transposed else (channels, LANES)
    channel = lax.broadcasted_iota(jnp.int32, shape, 1 if transposed else 0)
    lane = lax.broadcasted_iota(jnp.int32, shape, 0 if transposed else 1)
    low = (lane - offset) * span
    return ((channel >= low) & (channel < low + span)).astype(jnp.float32)


def exact_dot(a, one_hot):
    high = a.astype(jnp.bfloat16).astype(jnp.float32)
    rest = a - high
    middle = rest.astype(jnp.bfloat16).astype(jnp.float32)
    terms = jnp.concatenate([high, middle, rest - middle, jnp.zeros_like(a)], 0).astype(jnp.bfloat16)
    out = jnp.dot(terms, one_hot.astype(jnp.bfloat16), preferred_element_type=jnp.float32)
    return out[:8] + out[8:16] + out[16:24]


def merge(rows):
    totals = jnp.sum(rows, axis=0, keepdims=True)
    entries = pltpu.roll(totals, 3 * GROUPS, 1)
    mean = pltpu.roll(totals, 2 * GROUPS, 1) / entries
    off = rows - mean
    between = jnp.sum(pltpu.roll(rows, 3 * GROUPS, 1) * (off * off), axis=0, keepdims=True)
    return totals, mean, pltpu.roll(totals, GROUPS, 1) + between, entries


def as_row(totals, mean, spread):
    lane = lax.broadcasted_iota(jnp.int32, totals.shape, 1)
    row = jnp.where(lane // GROUPS == 1, pltpu.roll(spread, 3 * GROUPS, 1), totals)
    return jnp.where(lane // GROUPS == 2, mean, row)


def as_result(totals, mean, spread, entries):
    scale = lax.rsqrt(spread / entries + EPSILON)
    lane = lax.broadcasted_iota(jnp.int32, totals.shape, 1)
    return jnp.where(lane < 3 * GROUPS, mean, pltpu.roll(scale, GROUPS, 1))


def exchange_kernel(
    dims, features, weights_in, gain_in, shift_in, bias_in, counts, lengths,
    block, halo, stats, weights, gain, shift, bias,
    leaving, row, first, second, table, result,
    load_sem, weight_sem, row_send, direct_send, direct_sem, first_sem, second_send, second_sem,
    result_send, result_sem, halo_send, halo_sem,
):
    size_x, size_y, size_z, n_tm, n_tile = dims
    frames, height, width, channels = block.shape
    tm, tile = lax.axis_index("tm"), lax.axis_index("tile")
    x, core = tm // 2, tm % 2
    y, z = tile // size_z, tile % size_z
    planes, half = size_z // 2, size_z // 4
    gathers = z < planes
    serves = ((z == 1) | (z == planes - 1)) & (core == 1)
    server = jnp.where(z < planes + half, planes - 1, 1)

    def column(other_z, other_core):
        return x * 2 + other_core, y * size_z + other_z

    def far(dx, dy):
        return ((x + dx) % size_x) * 2 + core, ((y + dy) % size_y) * size_z + z

    def beside(dt, dr):
        return (tm + dt + n_tm) % n_tm, (tile + dr + n_tile) % n_tile

    def is_early(at_x, at_y, at_z):
        off_x = jnp.where(at_x > size_x // 2, size_x - at_x, at_x)
        off_y = jnp.where(at_y > size_y // 2, size_y - at_y, at_y)
        return off_x + off_y + at_z <= REACH

    early = is_early(x, y, z)
    direct = []
    for reach in range(REACH + 1):
        for at_z in range(size_z):
            for at_y in range(size_y):
                for at_x in range(size_x):
                    off = min(at_x, size_x - at_x) + min(at_y, size_y - at_y) + at_z
                    if off == reach:
                        place = at_y * size_z + at_z
                        direct = direct + [(2 * at_x + 1, place), (2 * at_x, place)]
    rank = tile * n_tm + tm
    n_devices = n_tm * n_tile

    far_steps = [(dx, dy) for dx in range(size_x) for dy in range(size_y)][1:]
    halo_steps = [(a, b) for a in (-1, 0, 1) for b in (-1, 0, 1) if (a, b) != (0, 0)]
    n_column, n_gather = 2 * size_z, 2 * planes

    load = pltpu.make_async_copy(features, block, load_sem)
    load.start()

    barrier = pltpu.get_barrier_semaphore()

    def greet(device):
        pl.semaphore_signal(barrier, inc=1, device_id=device, device_id_type=MESH)

    for step in halo_steps:
        greet(beside(*step))

    @pl.when(gathers)
    def _():
        for dz in range(size_z):
            for dc in range(2):
                if dz + dc:
                    greet(column((z + dz) % size_z, (core + dc) % 2))
        for step in far_steps:
            greet(far(*step))

    @pl.when(jnp.logical_not(gathers))
    def _():
        greet(column(server, 1))

    @pl.when(early)
    def _():
        by_tm = [(tm + i) % n_tm for i in range(n_tm)]
        by_y = [(y + i) % size_y * size_z for i in range(size_y)]
        by_z = [(z + i) % size_z for i in range(size_z)]
        for dz in sorted(range(size_z), key=lambda i: abs(2 * i - size_z)):
            for dy in sorted(range(size_y), key=lambda i: abs(2 * i - size_y)):
                place = by_y[dy] + by_z[dz]
                for dt in sorted(range(n_tm), key=lambda i: abs(2 * i - n_tm)):
                    if dz + dy + dt:
                        greet((by_tm[dt], place))

    fetch = pltpu.make_async_copy(weights_in, weights, weight_sem)
    fetch.start()

    load.wait()
    count_here = counts[0]
    length_here = lengths[0]

    cells = (count_here * length_here * (width * (channels // GROUPS))).astype(jnp.float32)
    spread_out = group_matrix(channels, 0, True)
    gather = group_matrix(channels, 0, False)

    def over_live(term):
        total = jnp.zeros((8, channels), jnp.float32)
        for f in range(frames):
            for r in range(height):
                live = (f < count_here) & (r < length_here)
                part = term(block[f, r].astype(jnp.float32))
                part = jnp.where(live, part, 0.0)
                total = total + sum(part[8 * i : 8 * i + 8] for i in range(width // 8))
        return jnp.sum(exact_dot(total, gather), axis=0, keepdims=True)

    sums = over_live(lambda v: v)
    centre = exact_dot(jnp.broadcast_to(sums / cells, (8, LANES)), spread_out)[:1]
    spread = over_live(lambda v: (v - centre) * (v - centre))
    lane = lax.broadcasted_iota(jnp.int32, sums.shape, 1)
    packed = jnp.where(lane < GROUPS, sums, pltpu.roll(spread, GROUPS, 1))
    means = pltpu.roll(sums / cells, 2 * GROUPS, 1)
    row[0] = jnp.where(lane < 2 * GROUPS, packed, jnp.where(lane < 3 * GROUPS, means, cells))
    own = z * 2 + core

    def send_row(device):
        pltpu.make_async_remote_copy(
            src_ref=row.at[0], dst_ref=first.at[own], send_sem=row_send, recv_sem=first_sem,
            device_id=device, device_id_type=MESH,
        ).start()

    def to_early(device):
        return pltpu.make_async_remote_copy(
            src_ref=row.at[0], dst_ref=table.at[rank], send_sem=direct_send,
            recv_sem=direct_sem, device_id=device, device_id_type=MESH,
        )

    def send_early():
        for device in direct:
            @pl.when(jnp.logical_not((tm == device[0]) & (tile == device[1])))
            def _():
                to_early(device).start()

    def sent_early(count):
        sent = table.at[pl.ds(0, count)]
        pltpu.make_async_copy(sent, sent, direct_send).wait()

    others = len(direct) - jnp.where(early, 1, 0)

    @pl.when(gathers)
    def _():
        known = n_gather - 1 + len(far_steps) + len(halo_steps)
        pl.semaphore_wait(barrier, known + others + jnp.where(serves, 4, 0))
        send_early()
        first[own] = row[0]
        for dz in range(planes):
            for dc in range(2):
                if dz + dc:
                    send_row(column((z + dz) % planes, (core + dc) % 2))

    @pl.when(jnp.logical_not(gathers))
    def _():
        pl.semaphore_wait(barrier, n_gather + others + len(halo_steps))
        send_early()
        for to_z in range(planes):
            for to_core in range(2):
                send_row(column(to_z, to_core))

    recent = jnp.maximum(count_here - 2, 0)
    last_row = jnp.maximum(length_here - 1, 0)
    top, low = 2 * height, 2 * height + frames + 2
    for k in range(2):
        for r in range(height):
            leaving[k * height + r] = block[recent + k, r]
        leaving[top + k] = block[recent + k, last_row]
        leaving[low + k] = block[recent + k, 0]
    for k in range(frames):
        leaving[top + 2 + k] = block[k, last_row]
        leaving[low + 2 + k] = block[k, 0]
    for start, size, step in (
        (top + 2, frames, (0, 1)), (low + 2, frames, (0, -1)),
        (top, 2, (1, 1)), (low, 2, (1, -1)), (0, top, (1, 0)),
    ):
        part = pl.ds(start, size)
        pltpu.make_async_remote_copy(
            src_ref=leaving.at[part], dst_ref=halo.at[part], send_sem=halo_send, recv_sem=halo_sem,
            device_id=beside(*step), device_id_type=MESH,
        ).start()
    for source, target in ((gain_in, gain), (shift_in, shift), (bias_in, bias)):
        small = pltpu.make_async_copy(source, target, load_sem)
        small.start()
        small.wait()
    widen = group_matrix(channels, 2 * GROUPS, True) + group_matrix(channels, 3 * GROUPS, True)

    def settle():
        fetch.wait()
        pltpu.make_async_copy(leaving, leaving, halo_send).wait()
        pltpu.make_async_copy(halo, halo, halo_sem).wait()

    def answers():
        base = jnp.where(z == 1, planes + half, planes)
        return [
            pltpu.make_async_remote_copy(
                src_ref=result.at[0], dst_ref=result.at[0], send_sem=result_send,
                recv_sem=result_sem, device_id=column(base + k // 2, k % 2), device_id_type=MESH,
            )
            for k in range(4)
        ]

    @pl.when(gathers)
    def _():
        sent = first.at[pl.ds(0, n_gather - 1)]
        pltpu.make_async_copy(sent, sent, row_send).wait()
        arrived = first.at[pl.ds(0, n_column - 1)]
        pltpu.make_async_copy(arrived, arrived, first_sem).wait()
        totals, mean, spread, entries = merge(first[...].reshape(n_column, LANES))
        second[0] = as_row(totals, mean, spread)

        def for_peers(act):
            for i, (dx, dy) in enumerate(far_steps):
                @pl.when(jnp.logical_not(is_early((x + dx) % size_x, (y + dy) % size_y, z)))
                def _():
                    act(pltpu.make_async_remote_copy(
                        src_ref=second.at[0], dst_ref=second.at[1 + i], send_sem=second_send,
                        recv_sem=second_sem, device_id=far(dx, dy), device_id_type=MESH,
                    ))

        for_peers(lambda copy: copy.start())
        settle()
        for plane in range(planes):
            spared = sum(1 for device in direct if device[0] % 2 and device[1] % size_z == plane)
            for mine in range(2 if spared else 1):
                @pl.when((z == plane) & (early if mine else jnp.logical_not(early)))
                def _():
                    sent = second.at[pl.ds(0, len(far_steps) - spared + mine)]
                    pltpu.make_async_copy(sent, sent, second_send).wait()

        @pl.when(early)
        def _():
            sent_early(len(direct) - 1)
            table[rank] = row[0]
            arrived = table.at[pl.ds(0, n_devices - 1)]
            pltpu.make_async_copy(arrived, arrived, direct_sem).wait()
            result[0] = as_result(*merge(table[...].reshape(n_devices, LANES)))

        @pl.when(jnp.logical_not(early))
        def _():
            sent_early(len(direct))
            arrived = second.at[pl.ds(1, len(far_steps))]
            pltpu.make_async_copy(arrived, arrived, second_sem).wait()
            result[0] = as_result(*merge(second[...].reshape(1 + len(far_steps), LANES)))

        @pl.when(serves)
        def _():
            for answer in answers():
                answer.start()

    @pl.when(jnp.logical_not(gathers))
    def _():
        sent = first.at[pl.ds(0, n_gather)]
        pltpu.make_async_copy(sent, sent, row_send).wait()
        sent_early(len(direct))
        settle()
        pltpu.make_async_copy(result.at[0], result.at[0], result_sem).wait()

    both = jnp.broadcast_to(result[0], (8, LANES))
    lane = lax.broadcasted_iota(jnp.int32, both.shape, 1)
    sub = lax.broadcasted_iota(jnp.int32, both.shape, 0)
    stats[...] = exact_dot(jnp.where(lane // GROUPS == sub + 2, both, 0.0), widen)

    @pl.when(serves)
    def _():
        sent = first.at[pl.ds(0, 4)]
        pltpu.make_async_copy(sent, sent, result_send).wait()


def convolve_kernel(
    n_tile, features, halo, stats, weights, gain, shift, bias, counts, lengths,
    out_hbm,
    out, stacked, q0, q1, q2, woven, hidden, out_sem,
):
    frames, height, width, channels = features.shape
    slots, run, depth = height + 2, frames * width, 3 * channels
    products = (q0, q1, q2)
    top, low = 2 * height, 2 * height + frames + 2
    tm, tile = lax.axis_index("tm"), lax.axis_index("tile")
    count_here = counts[0]
    length_here = lengths[0]
    mean = stats[0:1]
    scale = stats[1:2] * gain[...]
    offset = shift[...]
    column = lax.broadcasted_iota(jnp.int32, (width, 1), 0)

    def normalise(slot, k):
        is_lower = slot == length_here + 1
        blank = (slot == 0) & (tile == 0) | is_lower & (tile == n_tile - 1)
        frame = jnp.where(tm == 0, 2, k) if k < 2 else k
        if slot == 0:
            v = halo[top + frame]
        elif slot == slots - 1:
            v = halo[low + frame]
        else:
            v = halo[k * height + slot - 1] if k < 2 else features[k - 2, slot - 1]
            if k < 2:
                v = jnp.where(tm == 0, features[0, slot - 1], v)
            if slot > 1:
                v = jnp.where(is_lower, halo[low + frame], v)
        v = v.astype(jnp.float32)
        v = (v - mean) * scale + offset
        v = v / (1.0 + jnp.exp(-v))
        hidden[slot % 2, pl.ds(k * width, width)] = jnp.where(blank, 0.0, v)

    def stack(slot, a):
        stacked[pl.ds(slot * run, run), pl.ds(a * channels, channels)] = hidden[
            slot % 2, pl.ds(a * width, run)
        ].astype(jnp.bfloat16)

    def multiply(slot, h, v):
        kernel = weights[:, v, h].reshape(depth, weights.shape[-1])
        products[v][h, slot] = jnp.dot(
            stacked[pl.ds(slot * run, run)], kernel, preferred_element_type=jnp.float32
        )

    def finish(r, s, t):
        at = pl.ds(t * width, width)
        first, middle, last = [
            q0[h, r + s, at] + q1[h, r + 1, at] + q2[h, r + 1 + s, at] for h in range(3)
        ]
        middle = middle + bias[...]
        left = jnp.where(column == 0, 0.0, pltpu.roll(first, 1, 0))
        right = jnp.where(column == width - 1, 0.0, pltpu.roll(last, width - 1, 0))
        live = (t < count_here) & (r < length_here)
        even = jnp.where(live, middle + left + last, 0.0)
        odd = jnp.where(live, middle + right + first, 0.0)
        slab = (2 * r + s) * frames + t
        for i in range(even.shape[-1] // LANES):
            lanes = slice(i * LANES, (i + 1) * LANES)
            woven[slab, i, pl.ds(0, width, 2)] = even[:, lanes]
            woven[slab, i, pl.ds(1, width, 2)] = odd[:, lanes]
            out[t, 2 * r + s, :, lanes] = woven[slab, i].astype(jnp.bfloat16)

    def leave(row):
        return pltpu.make_async_copy(out.at[:, row], out_hbm.at[:, row], out_sem)

    def preparing(slot):
        work = [functools.partial(normalise, slot, k) for k in range(frames + 2)]
        return work + [functools.partial(stack, slot, a) for a in range(3)]

    def finishing(r, s):
        work = [functools.partial(finish, r, s, t) for t in range(frames)]
        return work + [lambda: leave(2 * r + s).start()]

    for piece in preparing(0):
        piece()
    for slot in range(slots):
        beside = preparing(slot + 1) if slot + 1 < slots else []
        if 2 <= slot:
            beside = beside + finishing(slot - 2, 0)
        if 3 <= slot:
            beside = finishing(slot - 3, 1) + beside
        taps = [
            (h, v) for h in range(3) for v in range(3)
            if not (slot == 0 and v > 0 or slot == slots - 1 and v < 2)
        ]
        done = 0
        for i, (h, v) in enumerate(taps):
            multiply(slot, h, v)
            upto = len(beside) * (i + 1) // len(taps)
            for piece in beside[done:upto]:
                piece()
            done = upto
    for piece in finishing(height - 1, 1):
        piece()
    pltpu.make_async_copy(out, out_hbm, out_sem).wait()


def body(dims, features, frame_counts, row_lengths, norm_gain, norm_shift, conv_weight, conv_bias):
    frames, height, width, channels = features.shape
    made = conv_weight.shape[-1]
    size_x, size_y, size_z, n_tm, n_tile = dims
    run = frames * width
    anywhere = pl.BlockSpec(memory_space=pl.ANY)
    in_vmem = pl.BlockSpec(memory_space=pltpu.VMEM)
    in_smem = pl.BlockSpec(memory_space=pltpu.SMEM)
    bf16, f32 = jnp.bfloat16, jnp.float32
    halo = (2 * height + 2 * (frames + 2), width, channels)
    ready = pl.pallas_call(
        functools.partial(exchange_kernel, dims),
        out_shape=(
            pltpu.VMEM(features.shape, bf16),
            pltpu.VMEM(halo, bf16),
            pltpu.VMEM((8, channels), f32),
            pltpu.VMEM(conv_weight.shape, bf16),
            pltpu.VMEM((1, channels), f32),
            pltpu.VMEM((1, channels), f32),
            pltpu.VMEM((1, made), f32),
        ),
        in_specs=[anywhere] * 5 + [in_smem] * 2,
        out_specs=(in_vmem,) * 7,
        scratch_shapes=[
            pltpu.VMEM(halo, bf16),
            pltpu.VMEM((1, 1, LANES), f32),
            pltpu.VMEM((size_z * 2, 1, LANES), f32),
            pltpu.VMEM((size_x * size_y, 1, LANES), f32),
            pltpu.VMEM((n_tm * n_tile, 1, LANES), f32),
            pltpu.VMEM((1, 1, LANES), f32),
        ]
        + [pltpu.SemaphoreType.DMA] * 12,
        compiler_params=pltpu.CompilerParams(
            collective_id=0, has_side_effects=True, vmem_limit_bytes=EXCHANGE_VMEM
        ),
        name="exchange",
    )(
        features, conv_weight, norm_gain.reshape(1, channels), norm_shift.reshape(1, channels),
        conv_bias.reshape(1, made), frame_counts, row_lengths,
    )
    return pl.pallas_call(
        functools.partial(convolve_kernel, n_tile),
        out_shape=jax.ShapeDtypeStruct((frames, 2 * height, 2 * width, made), bf16),
        in_specs=[in_vmem] * 7 + [in_smem] * 2,
        out_specs=anywhere,
        scratch_shapes=[
            pltpu.VMEM((frames, 2 * height, 2 * width, made), bf16),
            pltpu.VMEM(((height + 2) * run, 3 * channels), bf16),
            pltpu.VMEM((3, height + 2, run, made), f32),
            pltpu.VMEM((3, height + 2, run, made), f32),
            pltpu.VMEM((3, height + 2, run, made), f32),
            pltpu.VMEM((2 * height * frames, made // LANES, 2 * width, LANES), f32),
            pltpu.VMEM((2, (frames + 2) * width, channels), f32),
            pltpu.SemaphoreType.DMA,
        ],
        compiler_params=pltpu.CompilerParams(vmem_limit_bytes=CONVOLVE_VMEM),
        name="convolve",
    )(*ready, frame_counts, row_lengths)


def factors(mesh):
    n_tm, n_tile = mesh.shape["tm"], mesh.shape["tile"]
    size_y = 1
    while size_y * size_y * 2 < n_tile:
        size_y *= 2
    return n_tm // 2, size_y, n_tile // size_y, n_tm, n_tile


def solution(mesh):
    in_specs = (P("tm", "tile", None, None), P("tm"), P("tile"), P(), P(), P(), P())
    out_specs = P("tm", "tile", None, None)
    return jax.shard_map(
        functools.partial(body, factors(mesh)),
        mesh=mesh, in_specs=in_specs, out_specs=out_specs, check_vma=False,
    )
```

```python
import functools

import jax
import jax.numpy as jnp
from jax import lax
from jax.experimental import pallas as pl
from jax.experimental.pallas import tpu as pltpu
from jax.sharding import PartitionSpec as P

GROUPS = 32
REACH = 1
EPSILON = 1e-06
MESH = pl.DeviceIdType.MESH
LANES = 128
EXCHANGE_VMEM = 48 * 1024 * 1024
CONVOLVE_VMEM = 40 * 1024 * 1024


def group_matrix(channels, offset, transposed):
    span = channels // GROUPS
    shape = (LANES, channels) if transposed else (channels, LANES)
    channel = lax.broadcasted_iota(jnp.int32, shape, 1 if transposed else 0)
    lane = lax.broadcasted_iota(jnp.int32, shape, 0 if transposed else 1)
    low = (lane - offset) * span
    return ((channel >= low) & (channel < low + span)).astype(jnp.float32)


def exact_dot(a, one_hot):
    high = a.astype(jnp.bfloat16).astype(jnp.float32)
    rest = a - high
    middle = rest.astype(jnp.bfloat16).astype(jnp.float32)
    terms = jnp.concatenate([high, middle, rest - middle, jnp.zeros_like(a)], 0).astype(jnp.bfloat16)
    out = jnp.dot(terms, one_hot.astype(jnp.bfloat16), preferred_element_type=jnp.float32)
    return out[:8] + out[8:16] + out[16:24]


def merge(rows):
    totals = jnp.sum(rows, axis=0, keepdims=True)
    entries = pltpu.roll(totals, 3 * GROUPS, 1)
    mean = pltpu.roll(totals, 2 * GROUPS, 1) / entries
    off = rows - mean
    between = jnp.sum(pltpu.roll(rows, 3 * GROUPS, 1) * (off * off), axis=0, keepdims=True)
    return totals, mean, pltpu.roll(totals, GROUPS, 1) + between, entries


def as_row(totals, mean, spread):
    lane = lax.broadcasted_iota(jnp.int32, totals.shape, 1)
    row = jnp.where(lane // GROUPS == 1, pltpu.roll(spread, 3 * GROUPS, 1), totals)
    return jnp.where(lane // GROUPS == 2, mean, row)


def as_result(totals, mean, spread, entries):
    scale = lax.rsqrt(spread / entries + EPSILON)
    lane = lax.broadcasted_iota(jnp.int32, totals.shape, 1)
    return jnp.where(lane < 3 * GROUPS, mean, pltpu.roll(scale, GROUPS, 1))


def exchange_kernel(
    dims, features, weights_in, gain_in, shift_in, bias_in, counts, lengths,
    block, halo, stats, weights, gain, shift, bias,
    leaving, row, first, second, table, result,
    load_sem, weight_sem, row_send, direct_send, direct_sem, first_sem, second_send, second_sem,
    result_send, result_sem, halo_send, halo_sem,
):
    size_x, size_y, size_z, n_tm, n_tile = dims
    frames, height, width, channels = block.shape
    tm, tile = lax.axis_index("tm"), lax.axis_index("tile")
    x, core = tm // 2, tm % 2
    y, z = tile // size_z, tile % size_z
    planes, half = size_z // 2, size_z // 4
    gathers = z < planes
    serves = ((z == 1) | (z == planes - 1)) & (core == 1)
    server = jnp.where(z < planes + half, planes - 1, 1)

    def column(other_z, other_core):
        return x * 2 + other_core, y * size_z + other_z

    def far(dx, dy):
        return ((x + dx) % size_x) * 2 + core, ((y + dy) % size_y) * size_z + z

    def beside(dt, dr):
        return (tm + dt + n_tm) % n_tm, (tile + dr + n_tile) % n_tile

    def is_early(at_x, at_y, at_z):
        off_x = jnp.where(at_x > size_x // 2, size_x - at_x, at_x)
        off_y = jnp.where(at_y > size_y // 2, size_y - at_y, at_y)
        return off_x + off_y + at_z <= REACH

    early = is_early(x, y, z)
    direct = []
    for reach in range(REACH + 1):
        for at_z in range(size_z):
            for at_y in range(size_y):
                for at_x in range(size_x):
                    off = min(at_x, size_x - at_x) + min(at_y, size_y - at_y) + at_z
                    if off == reach:
                        place = at_y * size_z + at_z
                        direct = direct + [(2 * at_x + 1, place), (2 * at_x, place)]
    rank = tile * n_tm + tm
    n_devices = n_tm * n_tile

    far_steps = [(dx, dy) for dx in range(size_x) for dy in range(size_y)][1:]
    top, low = 2 * height, 2 * height + frames + 2
    parts = [
        (top + 2, frames, (0, 1)), (low + 2, frames, (0, -1)),
        (top, 2, (1, 1)), (low, 2, (1, -1)), (0, top, (1, 0)),
    ]

    def inside(dt, dr):
        return (tm + dt >= 0) & (tm + dt < n_tm) & (tile + dr >= 0) & (tile + dr < n_tile)

    halo_known = sum(jnp.where(inside(*step), 1, 0) for _, _, step in parts)
    n_column, n_gather = 2 * size_z, 2 * planes

    load = pltpu.make_async_copy(features, block, load_sem)
    load.start()

    barrier = pltpu.get_barrier_semaphore()

    def greet(device):
        pl.semaphore_signal(barrier, inc=1, device_id=device, device_id_type=MESH)

    for _, _, (dt, dr) in parts:
        @pl.when(inside(-dt, -dr))
        def _():
            greet(beside(-dt, -dr))

    @pl.when(gathers)
    def _():
        for dz in range(size_z):
            for dc in range(2):
                if dz + dc:
                    greet(column((z + dz) % size_z, (core + dc) % 2))
        for step in far_steps:
            greet(far(*step))

    @pl.when(jnp.logical_not(gathers))
    def _():
        greet(column(server, 1))

    @pl.when(early)
    def _():
        by_tm = [(tm + i) % n_tm for i in range(n_tm)]
        by_y = [(y + i) % size_y * size_z for i in range(size_y)]
        by_z = [(z + i) % size_z for i in range(size_z)]
        for dz in sorted(range(size_z), key=lambda i: abs(2 * i - size_z)):
            for dy in sorted(range(size_y), key=lambda i: abs(2 * i - size_y)):
                place = by_y[dy] + by_z[dz]
                for dt in sorted(range(n_tm), key=lambda i: abs(2 * i - n_tm)):
                    if dz + dy + dt:
                        greet((by_tm[dt], place))

    fetch = pltpu.make_async_copy(weights_in, weights, weight_sem)
    fetch.start()

    load.wait()
    count_here = counts[0]
    length_here = lengths[0]

    cells = (count_here * length_here * (width * (channels // GROUPS))).astype(jnp.float32)
    spread_out = group_matrix(channels, 0, True)
    gather = group_matrix(channels, 0, False)

    def over_live(term):
        total = jnp.zeros((8, channels), jnp.float32)
        for f in range(frames):
            for r in range(height):
                live = (f < count_here) & (r < length_here)
                part = term(block[f, r].astype(jnp.float32))
                part = jnp.where(live, part, 0.0)
                total = total + sum(part[8 * i : 8 * i + 8] for i in range(width // 8))
        return jnp.sum(exact_dot(total, gather), axis=0, keepdims=True)

    sums = over_live(lambda v: v)
    centre = exact_dot(jnp.broadcast_to(sums / cells, (8, LANES)), spread_out)[:1]
    spread = over_live(lambda v: (v - centre) * (v - centre))
    lane = lax.broadcasted_iota(jnp.int32, sums.shape, 1)
    packed = jnp.where(lane < GROUPS, sums, pltpu.roll(spread, GROUPS, 1))
    means = pltpu.roll(sums / cells, 2 * GROUPS, 1)
    row[0] = jnp.where(lane < 2 * GROUPS, packed, jnp.where(lane < 3 * GROUPS, means, cells))
    own = z * 2 + core

    def send_row(device):
        pltpu.make_async_remote_copy(
            src_ref=row.at[0], dst_ref=first.at[own], send_sem=row_send, recv_sem=first_sem,
            device_id=device, device_id_type=MESH,
        ).start()

    def to_early(device):
        return pltpu.make_async_remote_copy(
            src_ref=row.at[0], dst_ref=table.at[rank], send_sem=direct_send,
            recv_sem=direct_sem, device_id=device, device_id_type=MESH,
        )

    def send_early():
        for device in direct:
            @pl.when(jnp.logical_not((tm == device[0]) & (tile == device[1])))
            def _():
                to_early(device).start()

    def sent_early(count):
        sent = table.at[pl.ds(0, count)]
        pltpu.make_async_copy(sent, sent, direct_send).wait()

    others = len(direct) - jnp.where(early, 1, 0)

    @pl.when(gathers)
    def _():
        known = n_gather - 1 + len(far_steps) + halo_known
        pl.semaphore_wait(barrier, known + others + jnp.where(serves, 4, 0))
        send_early()
        first[own] = row[0]
        for dz in range(planes):
            for dc in range(2):
                if dz + dc:
                    send_row(column((z + dz) % planes, (core + dc) % 2))

    @pl.when(jnp.logical_not(gathers))
    def _():
        pl.semaphore_wait(barrier, n_gather + others + halo_known)
        send_early()
        for to_z in range(planes):
            for to_core in range(2):
                send_row(column(to_z, to_core))

    recent = jnp.maximum(count_here - 2, 0)
    last_row = jnp.maximum(length_here - 1, 0)
    for k in range(2):
        for r in range(height):
            leaving[k * height + r] = block[recent + k, r]
        leaving[top + k] = block[recent + k, last_row]
        leaving[low + k] = block[recent + k, 0]
    for k in range(frames):
        leaving[top + 2 + k] = block[k, last_row]
        leaving[low + 2 + k] = block[k, 0]
    halos = [
        pltpu.make_async_remote_copy(
            src_ref=leaving.at[pl.ds(start, size)], dst_ref=halo.at[pl.ds(start, size)],
            send_sem=halo_send.at[i], recv_sem=halo_sem.at[i],
            device_id=beside(*step), device_id_type=MESH,
        )
        for i, (start, size, step) in enumerate(parts)
    ]
    for copy, (_, _, step) in zip(halos, parts):
        @pl.when(inside(*step))
        def _():
            copy.start()

    for source, target in ((gain_in, gain), (shift_in, shift), (bias_in, bias)):
        small = pltpu.make_async_copy(source, target, load_sem)
        small.start()
        small.wait()
    widen = group_matrix(channels, 2 * GROUPS, True) + group_matrix(channels, 3 * GROUPS, True)

    def settle():
        fetch.wait()
        for copy, (_, _, (dt, dr)) in zip(halos, parts):
            @pl.when(inside(dt, dr))
            def _():
                copy.wait_send()

            @pl.when(inside(-dt, -dr))
            def _():
                copy.wait_recv()

    def answers():
        base = jnp.where(z == 1, planes + half, planes)
        return [
            pltpu.make_async_remote_copy(
                src_ref=result.at[0], dst_ref=result.at[0], send_sem=result_send,
                recv_sem=result_sem, device_id=column(base + k // 2, k % 2), device_id_type=MESH,
            )
            for k in range(4)
        ]

    @pl.when(gathers)
    def _():
        sent = first.at[pl.ds(0, n_gather - 1)]
        pltpu.make_async_copy(sent, sent, row_send).wait()
        arrived = first.at[pl.ds(0, n_column - 1)]
        pltpu.make_async_copy(arrived, arrived, first_sem).wait()
        totals, mean, spread, entries = merge(first[...].reshape(n_column, LANES))
        second[0] = as_row(totals, mean, spread)

        def for_peers(act):
            for i, (dx, dy) in enumerate(far_steps):
                @pl.when(jnp.logical_not(is_early((x + dx) % size_x, (y + dy) % size_y, z)))
                def _():
                    act(pltpu.make_async_remote_copy(
                        src_ref=second.at[0], dst_ref=second.at[1 + i], send_sem=second_send,
                        recv_sem=second_sem, device_id=far(dx, dy), device_id_type=MESH,
                    ))

        for_peers(lambda copy: copy.start())
        settle()
        for plane in range(planes):
            spared = sum(1 for device in direct if device[0] % 2 and device[1] % size_z == plane)
            for mine in range(2 if spared else 1):
                @pl.when((z == plane) & (early if mine else jnp.logical_not(early)))
                def _():
                    sent = second.at[pl.ds(0, len(far_steps) - spared + mine)]
                    pltpu.make_async_copy(sent, sent, second_send).wait()

        @pl.when(early)
        def _():
            sent_early(len(direct) - 1)
            table[rank] = row[0]
            arrived = table.at[pl.ds(0, n_devices - 1)]
            pltpu.make_async_copy(arrived, arrived, direct_sem).wait()
            result[0] = as_result(*merge(table[...].reshape(n_devices, LANES)))

        @pl.when(jnp.logical_not(early))
        def _():
            sent_early(len(direct))
            arrived = second.at[pl.ds(1, len(far_steps))]
            pltpu.make_async_copy(arrived, arrived, second_sem).wait()
            result[0] = as_result(*merge(second[...].reshape(1 + len(far_steps), LANES)))

        @pl.when(serves)
        def _():
            for answer in answers():
                answer.start()

    @pl.when(jnp.logical_not(gathers))
    def _():
        sent = first.at[pl.ds(0, n_gather)]
        pltpu.make_async_copy(sent, sent, row_send).wait()
        sent_early(len(direct))
        settle()
        pltpu.make_async_copy(result.at[0], result.at[0], result_sem).wait()

    both = jnp.broadcast_to(result[0], (8, LANES))
    lane = lax.broadcasted_iota(jnp.int32, both.shape, 1)
    sub = lax.broadcasted_iota(jnp.int32, both.shape, 0)
    stats[...] = exact_dot(jnp.where(lane // GROUPS == sub + 2, both, 0.0), widen)

    @pl.when(serves)
    def _():
        sent = first.at[pl.ds(0, 4)]
        pltpu.make_async_copy(sent, sent, result_send).wait()


def convolve_kernel(
    n_tile, features, halo, stats, weights, gain, shift, bias, counts, lengths,
    out_hbm,
    out, stacked, q0, q1, q2, woven, hidden, out_sem,
):
    frames, height, width, channels = features.shape
    slots, run, depth = height + 2, frames * width, 3 * channels
    products = (q0, q1, q2)
    top, low = 2 * height, 2 * height + frames + 2
    tm, tile = lax.axis_index("tm"), lax.axis_index("tile")
    count_here = counts[0]
    length_here = lengths[0]
    mean = stats[0:1]
    scale = stats[1:2] * gain[...]
    offset = shift[...]
    column = lax.broadcasted_iota(jnp.int32, (width, 1), 0)

    def normalise(slot, k):
        is_lower = slot == length_here + 1
        blank = (slot == 0) & (tile == 0) | is_lower & (tile == n_tile - 1)
        frame = jnp.where(tm == 0, 2, k) if k < 2 else k
        if slot == 0:
            v = halo[top + frame]
        elif slot == slots - 1:
            v = halo[low + frame]
        else:
            v = halo[k * height + slot - 1] if k < 2 else features[k - 2, slot - 1]
            if k < 2:
                v = jnp.where(tm == 0, features[0, slot - 1], v)
            if slot > 1:
                v = jnp.where(is_lower, halo[low + frame], v)
        v = v.astype(jnp.float32)
        v = (v - mean) * scale + offset
        v = v / (1.0 + jnp.exp(-v))
        hidden[slot % 2, pl.ds(k * width, width)] = jnp.where(blank, 0.0, v)

    def stack(slot, a):
        stacked[pl.ds(slot * run, run), pl.ds(a * channels, channels)] = hidden[
            slot % 2, pl.ds(a * width, run)
        ].astype(jnp.bfloat16)

    def multiply(slot, h, v):
        kernel = weights[:, v, h].reshape(depth, weights.shape[-1])
        products[v][h, slot] = jnp.dot(
            stacked[pl.ds(slot * run, run)], kernel, preferred_element_type=jnp.float32
        )

    def finish(r, s, t):
        at = pl.ds(t * width, width)
        first, middle, last = [
            q0[h, r + s, at] + q1[h, r + 1, at] + q2[h, r + 1 + s, at] for h in range(3)
        ]
        middle = middle + bias[...]
        left = jnp.where(column == 0, 0.0, pltpu.roll(first, 1, 0))
        right = jnp.where(column == width - 1, 0.0, pltpu.roll(last, width - 1, 0))
        live = (t < count_here) & (r < length_here)
        even = jnp.where(live, middle + left + last, 0.0)
        odd = jnp.where(live, middle + right + first, 0.0)
        slab = (2 * r + s) * frames + t
        for i in range(even.shape[-1] // LANES):
            lanes = slice(i * LANES, (i + 1) * LANES)
            woven[slab, i, pl.ds(0, width, 2)] = even[:, lanes]
            woven[slab, i, pl.ds(1, width, 2)] = odd[:, lanes]
            out[t, 2 * r + s, :, lanes] = woven[slab, i].astype(jnp.bfloat16)

    def leave(row):
        return pltpu.make_async_copy(out.at[:, row], out_hbm.at[:, row], out_sem)

    def preparing(slot):
        work = [functools.partial(normalise, slot, k) for k in range(frames + 2)]
        return work + [functools.partial(stack, slot, a) for a in range(3)]

    def finishing(r, s):
        work = [functools.partial(finish, r, s, t) for t in range(frames)]
        return work + [lambda: leave(2 * r + s).start()]

    for piece in preparing(0):
        piece()
    for slot in range(slots):
        beside = preparing(slot + 1) if slot + 1 < slots else []
        if 2 <= slot:
            beside = beside + finishing(slot - 2, 0)
        if 3 <= slot:
            beside = finishing(slot - 3, 1) + beside
        taps = [
            (h, v) for h in range(3) for v in range(3)
            if not (slot == 0 and v > 0 or slot == slots - 1 and v < 2)
        ]
        done = 0
        for i, (h, v) in enumerate(taps):
            multiply(slot, h, v)
            upto = len(beside) * (i + 1) // len(taps)
            for piece in beside[done:upto]:
                piece()
            done = upto
    for piece in finishing(height - 1, 1):
        piece()
    pltpu.make_async_copy(out, out_hbm, out_sem).wait()


def body(dims, features, frame_counts, row_lengths, norm_gain, norm_shift, conv_weight, conv_bias):
    frames, height, width, channels = features.shape
    made = conv_weight.shape[-1]
    size_x, size_y, size_z, n_tm, n_tile = dims
    run = frames * width
    anywhere = pl.BlockSpec(memory_space=pl.ANY)
    in_vmem = pl.BlockSpec(memory_space=pltpu.VMEM)
    in_smem = pl.BlockSpec(memory_space=pltpu.SMEM)
    bf16, f32 = jnp.bfloat16, jnp.float32
    halo = (2 * height + 2 * (frames + 2), width, channels)
    ready = pl.pallas_call(
        functools.partial(exchange_kernel, dims),
        out_shape=(
            pltpu.VMEM(features.shape, bf16),
            pltpu.VMEM(halo, bf16),
            pltpu.VMEM((8, channels), f32),
            pltpu.VMEM(conv_weight.shape, bf16),
            pltpu.VMEM((1, channels), f32),
            pltpu.VMEM((1, channels), f32),
            pltpu.VMEM((1, made), f32),
        ),
        in_specs=[anywhere] * 5 + [in_smem] * 2,
        out_specs=(in_vmem,) * 7,
        scratch_shapes=[
            pltpu.VMEM(halo, bf16),
            pltpu.VMEM((1, 1, LANES), f32),
            pltpu.VMEM((size_z * 2, 1, LANES), f32),
            pltpu.VMEM((size_x * size_y, 1, LANES), f32),
            pltpu.VMEM((n_tm * n_tile, 1, LANES), f32),
            pltpu.VMEM((1, 1, LANES), f32),
        ]
        + [pltpu.SemaphoreType.DMA] * 10
        + [pltpu.SemaphoreType.DMA((5,))] * 2,
        compiler_params=pltpu.CompilerParams(
            collective_id=0, has_side_effects=True, vmem_limit_bytes=EXCHANGE_VMEM
        ),
        name="exchange",
    )(
        features, conv_weight, norm_gain.reshape(1, channels), norm_shift.reshape(1, channels),
        conv_bias.reshape(1, made), frame_counts, row_lengths,
    )
    return pl.pallas_call(
        functools.partial(convolve_kernel, n_tile),
        out_shape=jax.ShapeDtypeStruct((frames, 2 * height, 2 * width, made), bf16),
        in_specs=[in_vmem] * 7 + [in_smem] * 2,
        out_specs=anywhere,
        scratch_shapes=[
            pltpu.VMEM((frames, 2 * height, 2 * width, made), bf16),
            pltpu.VMEM(((height + 2) * run, 3 * channels), bf16),
            pltpu.VMEM((3, height + 2, run, made), f32),
            pltpu.VMEM((3, height + 2, run, made), f32),
            pltpu.VMEM((3, height + 2, run, made), f32),
            pltpu.VMEM((2 * height * frames, made // LANES, 2 * width, LANES), f32),
            pltpu.VMEM((2, (frames + 2) * width, channels), f32),
            pltpu.SemaphoreType.DMA,
        ],
        compiler_params=pltpu.CompilerParams(vmem_limit_bytes=CONVOLVE_VMEM),
        name="convolve",
    )(*ready, frame_counts, row_lengths)


def factors(mesh):
    n_tm, n_tile = mesh.shape["tm"], mesh.shape["tile"]
    size_y = 1
    while size_y * size_y * 2 < n_tile:
        size_y *= 2
    return n_tm // 2, size_y, n_tile // size_y, n_tm, n_tile


def solution(mesh):
    in_specs = (P("tm", "tile", None, None), P("tm"), P("tile"), P(), P(), P(), P())
    out_specs = P("tm", "tile", None, None)
    return jax.shard_map(
        functools.partial(body, factors(mesh)),
        mesh=mesh, in_specs=in_specs, out_specs=out_specs, check_vma=False,
    )
```

```python
import functools

import jax
import jax.numpy as jnp
from jax import lax
from jax.experimental import pallas as pl
from jax.experimental.pallas import tpu as pltpu
from jax.sharding import PartitionSpec as P

GROUPS = 32
REACH = 1
EPSILON = 1e-06
MESH = pl.DeviceIdType.MESH
LANES = 128
EXCHANGE_VMEM = 48 * 1024 * 1024
CONVOLVE_VMEM = 40 * 1024 * 1024


def group_matrix(channels, offset, transposed):
    span = channels // GROUPS
    shape = (LANES, channels) if transposed else (channels, LANES)
    channel = lax.broadcasted_iota(jnp.int32, shape, 1 if transposed else 0)
    lane = lax.broadcasted_iota(jnp.int32, shape, 0 if transposed else 1)
    low = (lane - offset) * span
    return ((channel >= low) & (channel < low + span)).astype(jnp.float32)


def exact_dot(a, one_hot):
    high = a.astype(jnp.bfloat16).astype(jnp.float32)
    rest = a - high
    middle = rest.astype(jnp.bfloat16).astype(jnp.float32)
    terms = jnp.concatenate([high, middle, rest - middle, jnp.zeros_like(a)], 0).astype(jnp.bfloat16)
    out = jnp.dot(terms, one_hot.astype(jnp.bfloat16), preferred_element_type=jnp.float32)
    return out[:8] + out[8:16] + out[16:24]


def merge(rows):
    totals = jnp.sum(rows, axis=0, keepdims=True)
    entries = pltpu.roll(totals, 3 * GROUPS, 1)
    mean = pltpu.roll(totals, 2 * GROUPS, 1) / entries
    off = rows - mean
    between = jnp.sum(pltpu.roll(rows, 3 * GROUPS, 1) * (off * off), axis=0, keepdims=True)
    return totals, mean, pltpu.roll(totals, GROUPS, 1) + between, entries


def as_row(totals, mean, spread):
    lane = lax.broadcasted_iota(jnp.int32, totals.shape, 1)
    row = jnp.where(lane // GROUPS == 1, pltpu.roll(spread, 3 * GROUPS, 1), totals)
    return jnp.where(lane // GROUPS == 2, mean, row)


def as_result(totals, mean, spread, entries):
    scale = lax.rsqrt(spread / entries + EPSILON)
    lane = lax.broadcasted_iota(jnp.int32, totals.shape, 1)
    return jnp.where(lane < 3 * GROUPS, mean, pltpu.roll(scale, GROUPS, 1))


def exchange_kernel(
    dims, features, weights_in, gain_in, shift_in, bias_in, counts, lengths,
    block, halo, stats, weights, gain, shift, bias,
    leaving, row, first, second, table, result,
    load_sem, weight_sem, row_send, direct_send, direct_sem, first_sem, second_send, second_sem,
    result_send, result_sem, halo_send, halo_sem,
):
    size_x, size_y, size_z, n_tm, n_tile = dims
    frames, height, width, channels = block.shape
    tm, tile = lax.axis_index("tm"), lax.axis_index("tile")
    x, core = tm // 2, tm % 2
    y, z = tile // size_z, tile % size_z
    planes, half = size_z // 2, size_z // 4
    gathers = z < planes
    serves = ((z == 1) | (z == planes - 1)) & (core == 1)
    server = jnp.where(z < planes + half, planes - 1, 1)

    def column(other_z, other_core):
        return x * 2 + other_core, y * size_z + other_z

    def far(dx, dy):
        return ((x + dx) % size_x) * 2 + core, ((y + dy) % size_y) * size_z + z

    def beside(dt, dr):
        return (tm + dt + n_tm) % n_tm, (tile + dr + n_tile) % n_tile

    def is_early(at_x, at_y, at_z):
        off_x = jnp.where(at_x > size_x // 2, size_x - at_x, at_x)
        off_y = jnp.where(at_y > size_y // 2, size_y - at_y, at_y)
        return off_x + off_y + at_z <= REACH

    early = is_early(x, y, z)
    direct = []
    for reach in range(REACH + 1):
        for at_z in range(size_z):
            for at_y in range(size_y):
                for at_x in range(size_x):
                    off = min(at_x, size_x - at_x) + min(at_y, size_y - at_y) + at_z
                    if off == reach:
                        place = at_y * size_z + at_z
                        direct = direct + [(2 * at_x + 1, place), (2 * at_x, place)]
    rank = tile * n_tm + tm
    n_devices = n_tm * n_tile

    far_steps = [(dx, dy) for dx in range(size_x) for dy in range(size_y)][1:]
    top, low = 2 * height, 2 * height + frames + 2
    parts = [
        (top + 2, frames, (0, 1)), (low + 2, frames, (0, -1)),
        (top, 2, (1, 1)), (low, 2, (1, -1)), (0, top, (1, 0)),
    ]

    def inside(dt, dr):
        return (tm + dt >= 0) & (tm + dt < n_tm) & (tile + dr >= 0) & (tile + dr < n_tile)

    halo_known = sum(jnp.where(inside(*step), 1, 0) for _, _, step in parts)
    n_column, n_gather = 2 * size_z, 2 * planes

    load = pltpu.make_async_copy(features, block, load_sem)
    load.start()

    barrier = pltpu.get_barrier_semaphore()

    def greet(device):
        pl.semaphore_signal(barrier, inc=1, device_id=device, device_id_type=MESH)

    for _, _, (dt, dr) in parts:
        @pl.when(inside(-dt, -dr))
        def _():
            greet(beside(-dt, -dr))

    @pl.when(gathers)
    def _():
        for dz in range(size_z):
            for dc in range(2):
                if dz + dc:
                    greet(column((z + dz) % size_z, (core + dc) % 2))
        for step in far_steps:
            greet(far(*step))

    @pl.when(jnp.logical_not(gathers))
    def _():
        greet(column(server, 1))

    @pl.when(early)
    def _():
        by_tm = [(tm + i) % n_tm for i in range(n_tm)]
        by_y = [(y + i) % size_y * size_z for i in range(size_y)]
        by_z = [(z + i) % size_z for i in range(size_z)]
        for dz in sorted(range(size_z), key=lambda i: abs(2 * i - size_z)):
            for dy in sorted(range(size_y), key=lambda i: abs(2 * i - size_y)):
                place = by_y[dy] + by_z[dz]
                for dt in sorted(range(n_tm), key=lambda i: abs(2 * i - n_tm)):
                    if dz + dy + dt:
                        greet((by_tm[dt], place))

    fetch = pltpu.make_async_copy(weights_in, weights, weight_sem)
    fetch.start()

    load.wait()
    count_here = counts[0]
    length_here = lengths[0]

    cells = (count_here * length_here * (width * (channels // GROUPS))).astype(jnp.float32)
    spread_out = group_matrix(channels, 0, True)
    gather = group_matrix(channels, 0, False)

    def over_live(term):
        total = jnp.zeros((8, channels), jnp.float32)
        for f in range(frames):
            for r in range(height):
                live = (f < count_here) & (r < length_here)
                part = term(block[f, r].astype(jnp.float32))
                part = jnp.where(live, part, 0.0)
                total = total + sum(part[8 * i : 8 * i + 8] for i in range(width // 8))
        return jnp.sum(exact_dot(total, gather), axis=0, keepdims=True)

    sums = over_live(lambda v: v)
    centre = exact_dot(jnp.broadcast_to(sums / cells, (8, LANES)), spread_out)[:1]
    spread = over_live(lambda v: (v - centre) * (v - centre))
    lane = lax.broadcasted_iota(jnp.int32, sums.shape, 1)
    packed = jnp.where(lane < GROUPS, sums, pltpu.roll(spread, GROUPS, 1))
    means = pltpu.roll(sums / cells, 2 * GROUPS, 1)
    row[0] = jnp.where(lane < 2 * GROUPS, packed, jnp.where(lane < 3 * GROUPS, means, cells))
    own = z * 2 + core

    def send_row(device):
        pltpu.make_async_remote_copy(
            src_ref=row.at[0], dst_ref=first.at[own], send_sem=row_send, recv_sem=first_sem,
            device_id=device, device_id_type=MESH,
        ).start()

    def to_early(device):
        return pltpu.make_async_remote_copy(
            src_ref=row.at[0], dst_ref=table.at[rank], send_sem=direct_send,
            recv_sem=direct_sem, device_id=device, device_id_type=MESH,
        )

    def send_early():
        for device in direct:
            @pl.when(jnp.logical_not((tm == device[0]) & (tile == device[1])))
            def _():
                to_early(device).start()

    def sent_early(count):
        sent = table.at[pl.ds(0, count)]
        pltpu.make_async_copy(sent, sent, direct_send).wait()

    others = len(direct) - jnp.where(early, 1, 0)

    @pl.when(gathers)
    def _():
        known = n_gather - 1 + len(far_steps) + halo_known
        pl.semaphore_wait(barrier, known + others + jnp.where(serves, 4, 0))
        send_early()
        first[own] = row[0]
        for dz in range(planes):
            for dc in range(2):
                if dz + dc:
                    send_row(column((z + dz) % planes, (core + dc) % 2))

    @pl.when(jnp.logical_not(gathers))
    def _():
        pl.semaphore_wait(barrier, n_gather + others + halo_known)
        send_early()
        for to_z in range(planes):
            for to_core in range(2):
                send_row(column(to_z, to_core))

    recent = jnp.maximum(count_here - 2, 0)
    last_row = jnp.maximum(length_here - 1, 0)
    for k in range(2):
        for r in range(height):
            leaving[k * height + r] = block[recent + k, r]
        leaving[top + k] = block[recent + k, last_row]
        leaving[low + k] = block[recent + k, 0]
    for k in range(frames):
        leaving[top + 2 + k] = block[k, last_row]
        leaving[low + 2 + k] = block[k, 0]
    halos = [
        pltpu.make_async_remote_copy(
            src_ref=leaving.at[pl.ds(start, size)], dst_ref=halo.at[pl.ds(start, size)],
            send_sem=halo_send.at[i], recv_sem=halo_sem.at[i],
            device_id=beside(*step), device_id_type=MESH,
        )
        for i, (start, size, step) in enumerate(parts)
    ]
    for copy, (_, _, step) in zip(halos, parts):
        @pl.when(inside(*step))
        def _():
            copy.start()

    for source, target in ((gain_in, gain), (shift_in, shift), (bias_in, bias)):
        small = pltpu.make_async_copy(source, target, load_sem)
        small.start()
        small.wait()
    widen = group_matrix(channels, 2 * GROUPS, True) + group_matrix(channels, 3 * GROUPS, True)

    def settle():
        fetch.wait()
        for copy, (_, _, (dt, dr)) in zip(halos, parts):
            @pl.when(inside(dt, dr))
            def _():
                copy.wait_send()

            @pl.when(inside(-dt, -dr))
            def _():
                copy.wait_recv()

    def answers():
        base = jnp.where(z == 1, planes + half, planes)
        return [
            pltpu.make_async_remote_copy(
                src_ref=result.at[0], dst_ref=result.at[0], send_sem=result_send,
                recv_sem=result_sem, device_id=column(base + k // 2, k % 2), device_id_type=MESH,
            )
            for k in range(4)
        ]

    @pl.when(gathers)
    def _():
        sent = first.at[pl.ds(0, n_gather - 1)]
        pltpu.make_async_copy(sent, sent, row_send).wait()
        arrived = first.at[pl.ds(0, n_column - 1)]
        pltpu.make_async_copy(arrived, arrived, first_sem).wait()
        totals, mean, spread, entries = merge(first[...].reshape(n_column, LANES))
        second[0] = as_row(totals, mean, spread)

        def for_peers(act):
            for i, (dx, dy) in enumerate(far_steps):
                @pl.when(jnp.logical_not(is_early((x + dx) % size_x, (y + dy) % size_y, z)))
                def _():
                    act(pltpu.make_async_remote_copy(
                        src_ref=second.at[0], dst_ref=second.at[1 + i], send_sem=second_send,
                        recv_sem=second_sem, device_id=far(dx, dy), device_id_type=MESH,
                    ))

        for_peers(lambda copy: copy.start())
        settle()
        for plane in range(planes):
            spared = sum(1 for device in direct if device[0] % 2 and device[1] % size_z == plane)
            for mine in range(2 if spared else 1):
                @pl.when((z == plane) & (early if mine else jnp.logical_not(early)))
                def _():
                    sent = second.at[pl.ds(0, len(far_steps) - spared + mine)]
                    pltpu.make_async_copy(sent, sent, second_send).wait()

        @pl.when(early)
        def _():
            sent_early(len(direct) - 1)
            table[rank] = row[0]
            arrived = table.at[pl.ds(0, n_devices - 1)]
            pltpu.make_async_copy(arrived, arrived, direct_sem).wait()
            result[0] = as_result(*merge(table[...].reshape(n_devices, LANES)))

        @pl.when(jnp.logical_not(early))
        def _():
            sent_early(len(direct))
            arrived = second.at[pl.ds(1, len(far_steps))]
            pltpu.make_async_copy(arrived, arrived, second_sem).wait()
            result[0] = as_result(*merge(second[...].reshape(1 + len(far_steps), LANES)))

        @pl.when(serves)
        def _():
            for answer in answers():
                answer.start()

    @pl.when(jnp.logical_not(gathers))
    def _():
        sent = first.at[pl.ds(0, n_gather)]
        pltpu.make_async_copy(sent, sent, row_send).wait()
        sent_early(len(direct))
        settle()
        pltpu.make_async_copy(result.at[0], result.at[0], result_sem).wait()

    both = jnp.broadcast_to(result[0], (8, LANES))
    lane = lax.broadcasted_iota(jnp.int32, both.shape, 1)
    sub = lax.broadcasted_iota(jnp.int32, both.shape, 0)
    stats[...] = exact_dot(jnp.where(lane // GROUPS == sub + 2, both, 0.0), widen)

    @pl.when(serves)
    def _():
        sent = first.at[pl.ds(0, 4)]
        pltpu.make_async_copy(sent, sent, result_send).wait()


def convolve_kernel(
    n_tile, features, halo, stats, weights, gain, shift, bias, counts, lengths,
    out_hbm,
    out, stacked, q0, q1, q2, woven, hidden, out_sem,
):
    frames, height, width, channels = features.shape
    run, depth = frames * width, 3 * channels
    products = (q0, q1, q2)
    top, low = 2 * height, 2 * height + frames + 2
    tm, tile = lax.axis_index("tm"), lax.axis_index("tile")
    count_here = counts[0]
    length_here = lengths[0]
    mean = stats[0:1]
    scale = stats[1:2] * gain[...]
    offset = shift[...]
    column = lax.broadcasted_iota(jnp.int32, (width, 1), 0)

    def compute(live_rows, live_frames):
        slots, rows = live_rows + 2, live_frames * width

        def normalise(slot, k):
            frame = jnp.where(tm == 0, 2, k) if k < 2 else k
            blank = None
            if slot == 0:
                v, blank = halo[top + frame], tile == 0
            elif slot == slots - 1:
                v, blank = halo[low + frame], tile == n_tile - 1
            else:
                v = halo[k * height + slot - 1] if k < 2 else features[k - 2, slot - 1]
                if k < 2:
                    v = jnp.where(tm == 0, features[0, slot - 1], v)
            v = v.astype(jnp.float32)
            v = (v - mean) * scale + offset
            v = v / (1.0 + jnp.exp(-v))
            if blank is not None:
                v = jnp.where(blank, 0.0, v)
            hidden[slot % 2, pl.ds(k * width, width)] = v

        def stack(slot, a):
            stacked[pl.ds(slot * run, rows), pl.ds(a * channels, channels)] = hidden[
                slot % 2, pl.ds(a * width, rows)
            ].astype(jnp.bfloat16)

        def multiply(slot, h, v):
            kernel = weights[:, v, h].reshape(depth, weights.shape[-1])
            products[v][h, slot, pl.ds(0, rows)] = jnp.dot(
                stacked[pl.ds(slot * run, rows)], kernel, preferred_element_type=jnp.float32
            )

        def finish(r, s, t):
            at = pl.ds(t * width, width)
            first, middle, last = [
                q0[h, r + s, at] + q1[h, r + 1, at] + q2[h, r + 1 + s, at] for h in range(3)
            ]
            middle = middle + bias[...]
            left = jnp.where(column == 0, 0.0, pltpu.roll(first, 1, 0))
            right = jnp.where(column == width - 1, 0.0, pltpu.roll(last, width - 1, 0))
            live = t < count_here
            even = jnp.where(live, middle + left + last, 0.0)
            odd = jnp.where(live, middle + right + first, 0.0)
            slab = (2 * r + s) * frames + t
            for i in range(even.shape[-1] // LANES):
                lanes = slice(i * LANES, (i + 1) * LANES)
                woven[slab, i, pl.ds(0, width, 2)] = even[:, lanes]
                woven[slab, i, pl.ds(1, width, 2)] = odd[:, lanes]
                out[t, 2 * r + s, :, lanes] = woven[slab, i].astype(jnp.bfloat16)

        def leave(row):
            return pltpu.make_async_copy(out.at[:, row], out_hbm.at[:, row], out_sem)

        def preparing(slot):
            work = [functools.partial(normalise, slot, k) for k in range(live_frames + 2)]
            return work + [functools.partial(stack, slot, a) for a in range(3)]

        def finishing(r, s):
            work = [functools.partial(finish, r, s, t) for t in range(live_frames)]
            return work + [lambda: leave(2 * r + s).start()]

        for piece in preparing(0):
            piece()
        blank = jnp.zeros(out.shape[2:], out.dtype)
        for t in range(frames):
            for row in range(2 * height):
                if t >= live_frames or row >= 2 * live_rows:
                    out[t, row] = blank
        for row in range(2 * live_rows, 2 * height):
            leave(row).start()
        for slot in range(slots):
            beside = preparing(slot + 1) if slot + 1 < slots else []
            if 2 <= slot:
                beside = beside + finishing(slot - 2, 0)
            if 3 <= slot:
                beside = finishing(slot - 3, 1) + beside
            taps = [
                (h, v) for h in range(3) for v in range(3)
                if not (slot == 0 and v > 0 or slot == slots - 1 and v < 2)
            ]
            done = 0
            for i, (h, v) in enumerate(taps):
                multiply(slot, h, v)
                upto = len(beside) * (i + 1) // len(taps)
                for piece in beside[done:upto]:
                    piece()
                done = upto
        for piece in finishing(live_rows - 1, 1):
            piece()
        pltpu.make_async_copy(out, out_hbm, out_sem).wait()

    few_frames = count_here <= 4
    for live_rows in range(height, 0, -1):
        if live_rows == 1:
            right_rows = length_here <= 1
        elif live_rows == height:
            right_rows = length_here >= height
        else:
            right_rows = length_here == live_rows
        for live_frames in (frames, 4):
            @pl.when(right_rows & (few_frames if live_frames == 4 else jnp.logical_not(few_frames)))
            def _():
                compute(live_rows, live_frames)


def body(dims, features, frame_counts, row_lengths, norm_gain, norm_shift, conv_weight, conv_bias):
    frames, height, width, channels = features.shape
    made = conv_weight.shape[-1]
    size_x, size_y, size_z, n_tm, n_tile = dims
    run = frames * width
    anywhere = pl.BlockSpec(memory_space=pl.ANY)
    in_vmem = pl.BlockSpec(memory_space=pltpu.VMEM)
    in_smem = pl.BlockSpec(memory_space=pltpu.SMEM)
    bf16, f32 = jnp.bfloat16, jnp.float32
    halo = (2 * height + 2 * (frames + 2), width, channels)
    ready = pl.pallas_call(
        functools.partial(exchange_kernel, dims),
        out_shape=(
            pltpu.VMEM(features.shape, bf16),
            pltpu.VMEM(halo, bf16),
            pltpu.VMEM((8, channels), f32),
            pltpu.VMEM(conv_weight.shape, bf16),
            pltpu.VMEM((1, channels), f32),
            pltpu.VMEM((1, channels), f32),
            pltpu.VMEM((1, made), f32),
        ),
        in_specs=[anywhere] * 5 + [in_smem] * 2,
        out_specs=(in_vmem,) * 7,
        scratch_shapes=[
            pltpu.VMEM(halo, bf16),
            pltpu.VMEM((1, 1, LANES), f32),
            pltpu.VMEM((size_z * 2, 1, LANES), f32),
            pltpu.VMEM((size_x * size_y, 1, LANES), f32),
            pltpu.VMEM((n_tm * n_tile, 1, LANES), f32),
            pltpu.VMEM((1, 1, LANES), f32),
        ]
        + [pltpu.SemaphoreType.DMA] * 10
        + [pltpu.SemaphoreType.DMA((5,))] * 2,
        compiler_params=pltpu.CompilerParams(
            collective_id=0, has_side_effects=True, vmem_limit_bytes=EXCHANGE_VMEM
        ),
        name="exchange",
    )(
        features, conv_weight, norm_gain.reshape(1, channels), norm_shift.reshape(1, channels),
        conv_bias.reshape(1, made), frame_counts, row_lengths,
    )
    return pl.pallas_call(
        functools.partial(convolve_kernel, n_tile),
        out_shape=jax.ShapeDtypeStruct((frames, 2 * height, 2 * width, made), bf16),
        in_specs=[in_vmem] * 7 + [in_smem] * 2,
        out_specs=anywhere,
        scratch_shapes=[
            pltpu.VMEM((frames, 2 * height, 2 * width, made), bf16),
            pltpu.VMEM(((height + 2) * run, 3 * channels), bf16),
            pltpu.VMEM((3, height + 2, run, made), f32),
            pltpu.VMEM((3, height + 2, run, made), f32),
            pltpu.VMEM((3, height + 2, run, made), f32),
            pltpu.VMEM((2 * height * frames, made // LANES, 2 * width, LANES), f32),
            pltpu.VMEM((2, (frames + 2) * width, channels), f32),
            pltpu.SemaphoreType.DMA,
        ],
        compiler_params=pltpu.CompilerParams(vmem_limit_bytes=CONVOLVE_VMEM),
        name="convolve",
    )(*ready, frame_counts, row_lengths)


def factors(mesh):
    n_tm, n_tile = mesh.shape["tm"], mesh.shape["tile"]
    size_y = 1
    while size_y * size_y * 2 < n_tile:
        size_y *= 2
    return n_tm // 2, size_y, n_tile // size_y, n_tm, n_tile


def solution(mesh):
    in_specs = (P("tm", "tile", None, None), P("tm"), P("tile"), P(), P(), P(), P())
    out_specs = P("tm", "tile", None, None)
    return jax.shard_map(
        functools.partial(body, factors(mesh)),
        mesh=mesh, in_specs=in_specs, out_specs=out_specs, check_vma=False,
    )
```
